256 devices in a mesh: seq: 128 (over x_hi, z, y, core), head: 2 (over x_lo).
Axes of the slice: x: 4 (x_hi: 2, x_lo: 2; x = x_hi * 2 + x_lo), y: 4, z: 8, core: 2. Of those that a mesh axis runs over, the one named last changes fastest.
Arguments:
- inputs: bfloat16 [256, 128, 1152], P('seq'), may hold values from -8 to 8, as said below
- out_grad: bfloat16 [256, 128, 1152], P('seq'), may hold values from -6 to 6
- gate: float32 [1152], replicated, may hold values from -4 to 4
- qkv_weight: bfloat16 [1152, 3, 1152], P('seq', None, 'head'), as said below
- out_weight: bfloat16 [1152, 1152], P('seq', 'head'), may hold values from -0.1875 to 0.1875
Outputs:
- grad_inputs: bfloat16 [256, 128, 1152], P('seq')
- grad_qkv: float32 [1152, 3, 1152], P('seq', None, 'head')
- grad_out: float32 [1152, 1152], P('seq', 'head')
The draws below stay inside these ranges and needn't reach their ends.
Inputs may be any that keep to these rules, and one draw needn't show every extreme that they name: `inputs`: entries of the input tokens lie in this range. `qkv_weight`: entries lie within six times the fan-in scale 1 / sqrt(1152).
All inputs are finite; a program needn't handle non-finite values.
Results may differ from the reference program's by a relative error of at most 0.03.
The reference program's roundings to bfloat16 on the way count: a program that leaves them out, or rounds other values in their place, can miss the bound.
Values may be sent and summed in bfloat16 or wider, within the bound.
A program may use at most 128 MiB of HBM per device.

```python
import jax
import jax.numpy as jnp
from jax import lax

D = 1152
HEADS = 16
HEAD_DIM = 72
FRAMES = 32
S = 128
CLIPS = 8
TF = 256


def draw_inputs(key, part):
    key = jax.random.fold_in(key, 3)
    noise_key = jax.random.fold_in(key, 0)
    drawn = jnp.clip(jax.random.normal(noise_key, (TF, S, D), jnp.float32), -6.0, 6.0)
    return drawn.astype(jnp.bfloat16)


def draw_qkv_weight(key, part):
    key = jax.random.fold_in(key, 5)
    base_key = jax.random.fold_in(key, 0)
    base = jnp.clip(jax.random.normal(base_key, (D, 3, D), jnp.float32), -6.0, 6.0) * D ** (-0.5)
    return base.astype(jnp.bfloat16)


def shard_levels(stream_key, extent, cuts, low, high):
    gain = 1.0
    for dim, shards_of in cuts:
        draws = jax.random.uniform(jax.random.fold_in(jax.random.fold_in(stream_key, 6), dim), (shards_of,), jnp.float32, low / len(cuts), high / len(cuts))
        gain = gain * jnp.repeat(jnp.exp(draws), extent[dim] // shards_of).reshape((-1,) + (1,) * (len(extent) - 1 - dim))
    return gain


def bell_draw(stream_key, dims, width, most, cuts=(), held_as=jnp.bfloat16):
    factor_of = shard_levels(stream_key, dims, cuts, -0.22, 0.18) if cuts else 1.0
    drawn = jax.random.normal(stream_key, dims, jnp.float32) * width * factor_of
    return jnp.minimum(jnp.maximum(drawn, -most), most).astype(held_as)


def setup_inputs(seed: int = 0) -> dict:
    splits = jax.random.split(jax.random.key(seed), 6)
    return {
        "inputs": draw_inputs(jax.random.fold_in(splits[5], 71), 0),
        "out_grad": bell_draw(splits[1], (TF, S, D), 1.0, 6.0, ((0, 128),)),
        "gate": bell_draw(splits[2], (D,), 1.0, 4.0, (), jnp.float32),
        "qkv_weight": draw_qkv_weight(jax.random.fold_in(splits[5], 71), 0),
        "out_weight": bell_draw(splits[4], (D, D), D ** -0.5, 0.1875, ((0, 128), (1, 2))),
    }


def layer_norm(flat):
    mean = lax.optimization_barrier(jnp.mean(flat, -1, keepdims=True))
    centered = flat - mean
    rstd = lax.rsqrt(lax.optimization_barrier(jnp.mean(centered * centered, -1, keepdims=True)) + 1e-06)
    return (centered * rstd, rstd)

def attention_backward(query, keyed, value, dout):
    scale = HEAD_DIM ** (-0.5)
    qf = query.astype(jnp.float32)
    key_f = keyed.astype(jnp.float32)
    vf = value.astype(jnp.float32)
    df = dout.astype(jnp.float32)
    scores = jnp.einsum('fshe,gshe->shfg', qf, key_f) * scale
    probs = jax.nn.softmax(scores, axis=-1)
    probs_b = probs.astype(jnp.bfloat16)
    pbf = probs_b.astype(jnp.float32)
    attended = jnp.einsum('shfg,gshe->fshe', pbf, vf).astype(jnp.bfloat16)
    dprobs = jnp.einsum('fshe,gshe->shfg', df, vf)
    delta = jnp.einsum('fshe,fshe->shf', df, attended.astype(jnp.float32))
    dscores = (probs * (dprobs - delta[..., None]) * scale).astype(jnp.bfloat16)
    dsf = dscores.astype(jnp.float32)
    grad_q = jnp.einsum('shfg,gshe->fshe', dsf, key_f).astype(jnp.bfloat16)
    grad_k = jnp.einsum('shfg,fshe->gshe', dsf, qf).astype(jnp.bfloat16)
    grad_v = jnp.einsum('shfg,fshe->gshe', pbf, df).astype(jnp.bfloat16)
    return (grad_q, grad_k, grad_v, attended)

def reference(inputs, out_grad, gate, qkv_weight, out_weight):
    w_flat = qkv_weight.reshape(D, 3 * D)
    clip_in = inputs.reshape(CLIPS, FRAMES, S, D)
    clip_grad = out_grad.reshape(CLIPS, FRAMES, S, D)

    def one_clip(carry, pair):
        acc_qkv, acc_out = carry
        source, upstream = pair
        flat = source.reshape(-1, D).astype(jnp.float32)
        ghat, rstd = layer_norm(flat)
        normed = ghat.astype(jnp.bfloat16)
        up_flat = upstream.reshape(-1, D)
        gated = (gate * up_flat.astype(jnp.float32)).astype(jnp.bfloat16)
        qkv = jnp.dot(normed, w_flat, preferred_element_type=jnp.float32).astype(jnp.bfloat16)
        qkv = qkv.reshape(FRAMES, S, 3, HEADS, HEAD_DIM)
        dout = jnp.dot(gated, out_weight, preferred_element_type=jnp.float32).astype(jnp.bfloat16)
        dout = dout.reshape(FRAMES, S, HEADS, HEAD_DIM)
        grad_q, grad_k, grad_v, attended = attention_backward(qkv[:, :, 0], qkv[:, :, 1], qkv[:, :, 2], dout)
        dqkv = jnp.stack([grad_q, grad_k, grad_v], 2).reshape(-1, 3 * D)
        att_flat = attended.reshape(-1, D)
        acc_qkv = acc_qkv + lax.dot_general(normed, dqkv, (((0,), (0,)), ((), ())), preferred_element_type=jnp.float32)
        acc_out = acc_out + lax.dot_general(gated, att_flat, (((0,), (0,)), ((), ())), preferred_element_type=jnp.float32)
        dnormed = lax.dot_general(dqkv, w_flat, (((1,), (1,)), ((), ())), preferred_element_type=jnp.float32)
        dnormed = dnormed.astype(jnp.bfloat16).astype(jnp.float32)
        mean_one = lax.optimization_barrier(jnp.mean(dnormed, -1, keepdims=True))
        mean_two = lax.optimization_barrier(jnp.mean(dnormed * ghat, -1, keepdims=True))
        result = up_flat.astype(jnp.float32) + rstd * (dnormed - mean_one - ghat * mean_two)
        return ((acc_qkv, acc_out), result.astype(jnp.bfloat16).reshape(FRAMES, S, D))
    start = (jnp.zeros((D, 3 * D), jnp.float32), jnp.zeros((D, D), jnp.float32))
    (acc_qkv, acc_out), grads = lax.scan(one_clip, start, (clip_in, clip_grad))
    return (grads.reshape(TF, S, D), acc_qkv.reshape(D, 3, D), acc_out)
```

```python
import functools

import jax
import jax.numpy as jnp
from jax import lax
from jax.experimental import pallas as pl
from jax.experimental.pallas import tpu as pltpu
from jax.sharding import PartitionSpec as P

D = 1152
HEAD_DIM = 72
XS, ZS, YS = 2, 8, 4
CHIPS = XS * ZS * YS
BLK = 1408
MESH = pl.DeviceIdType.MESH
BF = jnp.bfloat16
F32 = jnp.float32
VMEM_BYTES = 58 * 2**20


def place():
    s = lax.axis_index("seq")
    h = lax.axis_index("head")
    return s // 64, (s // 8) % 8, (s // 2) % 4, s % 2, h


def seq_of(x, z, y, core):
    return ((x * 8 + z) * 4 + y) * 2 + core


def signal(sem, target):
    pl.semaphore_signal(sem, inc=1, device_id=target, device_id_type=MESH)


def remote(src, dst, send, recv, target):
    return pltpu.make_async_remote_copy(
        src_ref=src, dst_ref=dst, send_sem=send, recv_sem=recv, device_id=target, device_id_type=MESH
    )


def permuted_feature(shape, dim):
    f = lax.broadcasted_iota(jnp.int32, shape, dim)
    owner = f // 9
    q = f - owner * 9
    return jnp.where(q < 8, owner * 8 + q, 1024 + (owner % 2) * 64 + owner // 2)


def gather_kernel(
    in_ref, up_ref, wsh_ref, buf, xin,
    sib_v, mine_v, xg_v, perm_v,
    sib_sem, z_send, z_recv, x_sem, y_send, y_recv, t_send, t_recv, s_sem, l_sem,
):
    x, z, y, core, h = place()
    ck = (z % 2) * 4 + y
    sibling = (seq_of(x, z, y, 1 - core), h)
    x_peer = (seq_of(1 - x, z, y, core), h)
    z_peers = [(seq_of(x, (z + d) % 8, y, core), h) for d in range(1, 8)]
    y_peers = [(seq_of(x, z, (y + d) % 4, core), h) for d in range(1, 4)]
    t_chips = [(ck + d) % 8 for d in range(1, 8)]
    t_peers = [(seq_of(x, (z // 2) * 2 + c // 4, c % 4, core), h) for c in t_chips]
    everyone = [sibling, x_peer] + z_peers + y_peers + t_peers
    barrier = pltpu.get_barrier_semaphore()
    for peer in everyone:
        signal(barrier, peer)
    pl.semaphore_wait(barrier, len(everyone))

    swap = remote(wsh_ref.at[1 - core], sib_v, sib_sem.at[0], sib_sem.at[1], sibling)
    swap.start()
    swap.wait()
    mine_v[...] = wsh_ref[core] + sib_v[...]
    z_copies = [
        remote(mine_v, buf.at[x, z, y], z_send.at[d], z_recv.at[d], z_peers[d]) for d in range(7)
    ]
    for c in z_copies:
        c.start()
    own = pltpu.make_async_copy(mine_v, buf.at[x, z, y], l_sem.at[0])
    own.start()

    row = permuted_feature((D, 1), 0)
    col = lax.broadcasted_iota(jnp.int32, (1, D), 1)
    perm_v[...] = jnp.where(row == col, 1.0, 0.0).astype(BF)
    for i, ref in enumerate((in_ref, up_ref)):
        p = jnp.dot(ref[...].reshape(256, D), perm_v[...], preferred_element_type=F32)
        for g in range(16):
            part = jnp.concatenate([p[8 * g : 8 * g + 8], p[128 + 8 * g : 136 + 8 * g]], 0)
            xg_v[g, :, i * D : (i + 1) * D] = part.astype(BF)
    t_copies = [
        remote(
            xg_v.at[pl.ds(2 * t_chips[d], 2)], xin.at[:, ck, core],
            t_send.at[d], t_recv.at[d], t_peers[d],
        )
        for d in range(7)
    ]
    for c in t_copies:
        c.start()
    own_t = pltpu.make_async_copy(xg_v.at[pl.ds(2 * ck, 2)], xin.at[:, ck, core], l_sem.at[1])
    own_t.start()

    own.wait()
    for c in z_copies:
        c.wait()
    x_copy = remote(buf.at[x, :, y], buf.at[x, :, y], x_sem.at[0], x_sem.at[1], x_peer)
    x_copy.start()
    y_one = [
        remote(buf.at[x, :, y], buf.at[x, :, y], y_send.at[d], y_recv.at[d], y_peers[d])
        for d in range(3)
    ]
    for c in y_one:
        c.start()
    x_copy.wait()
    y_two = [
        remote(
            buf.at[1 - x, :, y], buf.at[1 - x, :, y], y_send.at[3 + d], y_recv.at[3 + d], y_peers[d]
        )
        for d in range(3)
    ]
    for c in y_two:
        c.start()
    own_t.wait()
    for c in t_copies:
        c.wait()
    s_copy = remote(xin.at[:, :, core], xin.at[:, :, core], s_sem.at[0], s_sem.at[1], sibling)
    s_copy.start()
    for c in y_one + y_two:
        c.wait()
    s_copy.wait()


def normalise(v):
    mean = jnp.mean(v, -1, keepdims=True)
    centered = v - mean
    rstd = lax.rsqrt(jnp.mean(centered * centered, -1, keepdims=True) + 1e-06)
    return centered * rstd, rstd


def turn(v, by):
    return jnp.concatenate([v[:, -by:], v[:, :-by]], 1)


def nt(a, b):
    return lax.dot_general(a, b, (((1,), (1,)), ((), ())), preferred_element_type=F32)


def tn(a, b):
    return lax.dot_general(a, b, (((0,), (0,)), ((), ())), preferred_element_type=F32)


def attention(qa, ka, va, da):
    scale = HEAD_DIM ** (-0.5)
    rows = lax.broadcasted_iota(jnp.int32, (256, 256), 0)
    cols = lax.broadcasted_iota(jnp.int32, (256, 256), 1)
    same = (rows & 7) == (cols & 7)
    outs = [[[] for _ in range(3)] for _ in range(4)]
    for head, (lo, hi) in enumerate(((0, 128), (0, 256), (128, 256), (128, 384))):
        lane = lax.broadcasted_iota(jnp.int32, (1, hi - lo), 1) + lo
        keep = (lane >= HEAD_DIM * head) & (lane < HEAD_DIM * (head + 1))
        q, k, v, d = (a[:, lo:hi] for a in (qa, ka, va, da))
        qm = jnp.where(keep, q, jnp.zeros_like(q))
        dm = jnp.where(keep, d, jnp.zeros_like(d))
        scores = jnp.where(same, nt(qm, k) * scale, -1e30)
        top = jnp.max(scores, -1, keepdims=True)
        e = jnp.exp(scores - top)
        probs = e / jnp.sum(e, -1, keepdims=True)
        probs_b = probs.astype(BF)
        att = jnp.dot(probs_b, v, preferred_element_type=F32).astype(BF)
        delta = jnp.sum(dm.astype(F32) * att.astype(F32), -1, keepdims=True)
        ds = (probs * (nt(dm, v) - delta) * scale).astype(BF)
        dq = jnp.dot(ds, k, preferred_element_type=F32)
        dk = tn(ds, q)
        dv = tn(probs_b, d)
        for slot, val in zip(outs, (dq, dk, dv, att.astype(F32))):
            val = jnp.where(keep, val, 0.0)
            for t in range(lo // 128, hi // 128):
                slot[t].append(val[:, t * 128 - lo : t * 128 - lo + 128])
    return [jnp.concatenate([functools.reduce(lambda a, b: a + b, t) for t in s], 1) for s in outs]


def compute_kernel(buf, xin, gate_ref, dw, dn, w_v, norm_v, dz_v, g_v, f_v):
    w_v[0:1024, :] = buf[:, :, 0:D].reshape(1024, D)
    for r in range(2):
        f_v[...] = buf[:, :, D + 128 * r : D + 128 * (r + 1)].reshape(1024, 128).astype(F32)
        for j in range(9):
            w_v[1024 + 64 * r : 1088 + 64 * r, 128 * j : 128 * (j + 1)] = f_v[
                pl.ds(j, 64, stride=16), :
            ].astype(BF)

    lane = lax.broadcasted_iota(jnp.int32, (1, 896), 1)

    def one(pg, carry):
        tok = pl.ds(pg * 256, 256)
        src = xin[pg].reshape(256, 2 * D)
        ghat, _ = normalise(src[:, :D].astype(F32))
        normed = ghat.astype(BF)
        norm_v[tok, :] = normed
        dz = (gate_ref[...] * src[:, D:].astype(F32)).astype(BF)
        dz_v[tok, :] = dz
        qkv = jnp.dot(normed, w_v[:, 0:896], preferred_element_type=F32)
        od = jnp.dot(dz, w_v[:, 768:1152], preferred_element_type=F32)
        qa = qkv[:, 0:384].astype(BF)
        ka = turn(qkv[:, 256:640], -32).astype(BF)
        va = turn(qkv[:, 512:896], -64).astype(BF)
        da = turn(od, -96).astype(BF)
        dq, dk, dv, att = attention(qa, ka, va, da)
        dk, dv, att = turn(dk, 32), turn(dv, 64), turn(att, 96)
        tiles = [[] for _ in range(9)]
        for start, val in ((0, dq), (2, dk), (4, dv), (6, att)):
            for t in range(3):
                tiles[start + t].append(val[:, 128 * t : 128 * (t + 1)])
        for t in range(9):
            g_v[tok, 128 * t : 128 * (t + 1)] = functools.reduce(lambda a, b: a + b, tiles[t]).astype(BF)
        left = jnp.where(lane < 864, g_v[tok, 0:896], jnp.zeros((256, 896), BF))
        dn[pg] = nt(left, w_v[:, 0:896]).astype(BF)
        return carry

    lax.fori_loop(0, 2, one, 0)

    def grads(i):
        c = slice(128 * i, 128 * (i + 1))
        a = tn(norm_v[:, c], g_v[:, 0:896])
        b = tn(dz_v[:, c], g_v[:, 768:1152])
        lane = lax.broadcasted_iota(jnp.int32, (1, 128), 1)
        mid = jnp.where(lane < 96, a[:, 768:896], b[:, 0:128])
        return jnp.concatenate([a[:, 0:768], mid, b[:, 128:384]], 1)

    for i in range(8):
        dw[8 * i : 8 * i + 8, :, 0:D] = grads(i).astype(BF).reshape(8, 16, D)
    rest = grads(8)
    for r in range(2):
        f_v[...] = jnp.zeros((1024, 128), F32)
        for j in range(9):
            f_v[pl.ds(j, 64, stride=16), :] = rest[64 * r : 64 * r + 64, 128 * j : 128 * (j + 1)]
        dw[:, :, D + 128 * r : D + 128 * (r + 1)] = f_v[...].astype(BF).reshape(64, 16, 128)


def scatter_kernel(
    dw, dn, xin, gw, out,
    own_y, ry, py, rx, px, rz, g_v, gs_v, dn_own, rs, ps, rh, xi_v, res_v, og, perm_v,
    y_send, y_recv, x_sem, z_send, z_recv, g_sem, s_sem, h_sem, o_send, o_recv, l_sem,
):
    x, z, y, core, h = place()
    zl = z % 2
    ck = zl * 4 + y
    member = ck * 2 + core
    sibling = (seq_of(x, z, y, 1 - core), h)
    x_peer = (seq_of(1 - x, z, y, core), h)
    h_peer = (seq_of(x, z, y, core), 1 - h)
    z_peers = [(seq_of(x, (z + d) % 8, y, core), h) for d in range(1, 8)]
    y_peers = [(seq_of(x, z, (y + d) % 4, core), h) for d in range(1, 4)]
    base = (x * 8 + (z // 2) * 2) * 8
    group = [(base + (member + i) % 16, (h + k) % 2) for i in range(16) for k in range(2)][1:]
    everyone = [x_peer] + z_peers + group
    barrier = pltpu.get_barrier_semaphore()
    for peer in everyone:
        signal(barrier, peer)
    pl.semaphore_wait(barrier, len(everyone))

    swap = remote(dn.at[1 - core], rs, s_sem.at[0], s_sem.at[1], sibling)
    swap.start()
    y_copies = [
        remote(dw.at[:, :, (y + d) % 4], ry.at[d - 1], y_send.at[d - 1], y_recv.at[d - 1], y_peers[d - 1])
        for d in range(1, 4)
    ]
    for c in y_copies:
        c.start()
    keep = pltpu.make_async_copy(dn.at[core], dn_own, l_sem.at[0])
    keep.start()
    keep_y = pltpu.make_async_copy(dw.at[:, :, y], own_y, l_sem.at[1])
    keep_y.start()
    tokens = pltpu.make_async_copy(xin.at[core, pl.ds(4 * h, 4)], xi_v, l_sem.at[2])
    tokens.start()
    row = lax.broadcasted_iota(jnp.int32, (D, 1), 0)
    perm_v[...] = jnp.where(row == permuted_feature((1, D), 1), 1.0, 0.0).astype(BF)
    keep.wait()
    swap.wait()
    ps[...] = (dn_own[...].astype(F32) + rs[...].astype(F32)).astype(BF)
    half = remote(ps.at[pl.ds((1 - h) * 128, 128)], rh, h_sem.at[0], h_sem.at[1], h_peer)
    half.start()
    tokens.wait()
    src = xi_v[...].reshape(128, 2 * D)
    ghat, rstd = normalise(src[:, :D].astype(F32))
    half.wait()
    mine = ps[pl.ds(pl.multiple_of(h * 128, 128), 128), :].astype(F32) + rh[...].astype(F32)
    mine = mine.astype(BF).astype(F32)
    one = jnp.mean(mine, -1, keepdims=True)
    two = jnp.mean(mine * ghat, -1, keepdims=True)
    res = src[:, D:].astype(F32) + rstd * (mine - one - ghat * two)
    res_v[...] = res.astype(BF).reshape(8, 16, D)
    o_copies = []
    for i in range(8):
        for k in range(2):
            o_copies.append((i, k))

    def send_out(i, k):
        to = lax.rem(member + i, 8)
        target = (base + 8 * h + to, (h + k) % 2)
        return remote(res_v.at[to], og.at[member], o_send.at[2 * i + k], o_recv.at[member], target)

    local = zl == h
    for i, k in o_copies:
        if i == 0 and k == 0:
            @pl.when(jnp.logical_not(local))
            def _():
                send_out(0, 0).start()

            @pl.when(local)
            def _():
                pltpu.make_async_copy(res_v.at[lax.rem(member, 8)], og.at[member], l_sem.at[3]).start()
        else:
            send_out(i, k).start()

    keep_y.wait()
    for c in y_copies:
        c.wait()

    def add_y(xx):
        t = own_y[xx].astype(F32)
        for d in range(3):
            t = t + ry[d, xx].astype(F32)
        py[xx] = t.astype(BF)

    add_y(1 - x)
    x_copy = remote(py.at[1 - x], rx, x_sem.at[0], x_sem.at[1], x_peer)
    x_copy.start()
    add_y(x)
    x_copy.wait()
    px[...] = (py[x].astype(F32) + rx[...].astype(F32)).astype(BF)
    z_copies = [
        remote(px.at[(z + d) % 8], rz.at[d - 1], z_send.at[d - 1], z_recv.at[d - 1], z_peers[d - 1])
        for d in range(1, 8)
    ]
    for c in z_copies:
        c.start()
    for c in z_copies:
        c.wait()
    t = px[z].astype(F32)
    for d in range(7):
        t = t + rz[d].astype(F32)
    g_v[...] = t
    g_copy = remote(g_v, gs_v, g_sem.at[0], g_sem.at[1], sibling)
    g_copy.start()

    for i, k in o_copies:
        if i == 0 and k == 0:
            @pl.when(jnp.logical_not(local))
            def _():
                send_out(0, 0).wait_send()

            @pl.when(local)
            def _():
                pltpu.make_async_copy(res_v.at[lax.rem(member, 8)], og.at[member], l_sem.at[3]).wait()
        else:
            send_out(i, k).wait_send()
    for m in range(16):
        @pl.when(jnp.logical_not(local & (member == m)))
        def _():
            remote(res_v.at[0], og.at[m], o_send.at[0], o_recv.at[m], h_peer).wait_recv()

    back = jnp.dot(og[...].reshape(256, D), perm_v[...], preferred_element_type=F32)
    for f in range(2):
        for g in range(8):
            a = back[32 * g + 8 * f : 32 * g + 8 * f + 8]
            b = back[32 * g + 16 + 8 * f : 32 * g + 24 + 8 * f]
            out[f, 16 * g : 16 * g + 16, :] = jnp.concatenate([a, b], 0).astype(BF)
    g_copy.wait()
    gw[core] = g_v[...]
    gw[1 - core] = gs_v[...]


def on_device(inputs, out_grad, gate, qkv_weight, out_weight):
    core = lax.axis_index("seq") % 2
    vm = pl.BlockSpec(memory_space=pltpu.VMEM)
    hbm = pl.BlockSpec(memory_space=pl.ANY)
    dma = pltpu.SemaphoreType.DMA

    w = jnp.concatenate([qkv_weight, out_weight[:, None]], 1).reshape(9, 4, 2, 288)
    w = w.transpose(2, 0, 1, 3).reshape(2, 9, D)
    main = w[:, :8]
    last = jnp.pad(w[:, 8].reshape(2, 9, 128), ((0, 0), (0, 7), (0, 0)))
    zero = jnp.zeros_like
    main = jnp.where(
        core == 0, jnp.concatenate([main, zero(main)], 1), jnp.concatenate([zero(main), main], 1)
    )
    last = jnp.where(
        core == 0, jnp.concatenate([last, zero(last)], 2), jnp.concatenate([zero(last), last], 2)
    )
    wsh = jnp.concatenate([main, last], 2)

    buf, xin = pl.pallas_call(
        gather_kernel,
        out_shape=[
            jax.ShapeDtypeStruct((XS, ZS, YS, 16, BLK), BF),
            jax.ShapeDtypeStruct((2, 8, 2, 16, 2 * D), BF),
        ],
        in_specs=[vm] * 3,
        out_specs=[hbm, hbm],
        scratch_shapes=[
            pltpu.VMEM((16, BLK), BF), pltpu.VMEM((16, BLK), BF),
            pltpu.VMEM((16, 16, 2 * D), BF), pltpu.VMEM((D, D), BF),
            dma((2,)), dma((7,)), dma((7,)), dma((2,)), dma((6,)), dma((6,)),
            dma((7,)), dma((7,)), dma((2,)), dma((2,)),
        ],
        compiler_params=pltpu.CompilerParams(
            collective_id=0, has_side_effects=True, vmem_limit_bytes=VMEM_BYTES
        ),
        name="gather",
    )(inputs, out_grad, wsh)

    gate_p = jnp.concatenate([gate.reshape(128, 9)[:, :8].reshape(1024), gate.reshape(64, 2, 9)[:, :, 8].T.reshape(128)])
    dw, dn = pl.pallas_call(
        compute_kernel,
        out_shape=[
            jax.ShapeDtypeStruct((CHIPS, 16, BLK), BF),
            jax.ShapeDtypeStruct((2, 256, D), BF),
        ],
        in_specs=[vm] * 3,
        out_specs=[vm, vm],
        scratch_shapes=[
            pltpu.VMEM((D, D), BF), pltpu.VMEM((512, D), BF), pltpu.VMEM((512, D), BF),
            pltpu.VMEM((512, D), BF), pltpu.VMEM((1024, 128), F32),
        ],
        compiler_params=pltpu.CompilerParams(vmem_limit_bytes=VMEM_BYTES),
        name="compute",
    )(buf.reshape(CHIPS, 16, BLK), xin, gate_p.reshape(1, D))

    gw, grad_inputs = pl.pallas_call(
        scatter_kernel,
        out_shape=[
            jax.ShapeDtypeStruct((2, 16, BLK), F32),
            jax.ShapeDtypeStruct((2, 128, D), BF),
        ],
        in_specs=[hbm] * 3,
        out_specs=[vm, vm],
        scratch_shapes=[
            pltpu.VMEM((XS, ZS, 16, BLK), BF), pltpu.VMEM((3, XS, ZS, 16, BLK), BF),
            pltpu.VMEM((XS, ZS, 16, BLK), BF), pltpu.VMEM((ZS, 16, BLK), BF),
            pltpu.VMEM((ZS, 16, BLK), BF), pltpu.VMEM((7, 16, BLK), BF),
            pltpu.VMEM((16, BLK), F32), pltpu.VMEM((16, BLK), F32),
            pltpu.VMEM((256, D), BF), pltpu.VMEM((256, D), BF), pltpu.VMEM((256, D), BF),
            pltpu.VMEM((128, D), BF), pltpu.VMEM((4, 2, 16, 2 * D), BF),
            pltpu.VMEM((8, 16, D), BF), pltpu.VMEM((16, 16, D), BF), pltpu.VMEM((D, D), BF),
            dma((3,)), dma((3,)), dma((2,)), dma((7,)), dma((7,)), dma((2,)), dma((2,)), dma((2,)),
            dma((16,)), dma((16,)), dma((4,)),
        ],
        compiler_params=pltpu.CompilerParams(
            collective_id=1, has_side_effects=True, vmem_limit_bytes=VMEM_BYTES
        ),
        name="scatter",
    )(dw.reshape(XS, ZS, YS, 16, BLK), dn, xin)

    main = jnp.where(core == 0, gw[:, 0:8, :D], gw[:, 8:16, :D])
    last = jnp.where(core == 0, gw[:, 0:9, D : D + 128], gw[:, 0:9, D + 128 :]).reshape(2, 1, D)
    full = jnp.concatenate([main, last], 1).reshape(2, 9, 4, 288).transpose(1, 2, 0, 3)
    full = full.reshape(9, 4, 576)
    return grad_inputs, full[:, 0:3], full[:, 3]


def solution(mesh):
    in_specs = (
        P("seq", None, None),
        P("seq", None, None),
        P(),
        P("seq", None, "head"),
        P("seq", "head"),
    )
    out_specs = (P("seq", None, None), P("seq", None, "head"), P("seq", "head"))
    return jax.shard_map(
        on_device, mesh=mesh, in_specs=in_specs, out_specs=out_specs, check_vma=False
    )
```

```python
import functools

import jax
import jax.numpy as jnp
from jax import lax
from jax.experimental import pallas as pl
from jax.experimental.pallas import tpu as pltpu
from jax.sharding import PartitionSpec as P

D = 1152
HEAD_DIM = 72
XS, ZS, YS = 2, 8, 4
CHIPS = XS * ZS * YS
BLK = 1408
PW = 512
RW = BLK - PW
RM = D - PW
MESH = pl.DeviceIdType.MESH
BF = jnp.bfloat16
F32 = jnp.float32
VMEM_BYTES = 58 * 2**20


def place():
    s = lax.axis_index("seq")
    h = lax.axis_index("head")
    return s // 64, (s // 8) % 8, (s // 2) % 4, s % 2, h


def seq_of(x, z, y, core):
    return ((x * 8 + z) * 4 + y) * 2 + core


def signal(sem, target):
    pl.semaphore_signal(sem, inc=1, device_id=target, device_id_type=MESH)


def remote(src, dst, send, recv, target):
    return pltpu.make_async_remote_copy(
        src_ref=src, dst_ref=dst, send_sem=send, recv_sem=recv, device_id=target, device_id_type=MESH
    )


def permuted_feature(shape, dim):
    f = lax.broadcasted_iota(jnp.int32, shape, dim)
    owner = f // 9
    q = f - owner * 9
    return jnp.where(q < 8, owner * 8 + q, 1024 + (owner % 2) * 64 + owner // 2)


class Copies:
    def __init__(self, send, recv):
        self.send, self.recv, self.count = send, recv, 0

    def start(self, src, dst, target):
        k = self.count
        self.count += 1
        c = remote(src, dst, self.send.at[k], self.recv.at[k], target)
        c.start()
        return c


def gather_kernel(
    in_ref, up_ref, wsh_ref, buf_p, buf_r, xin,
    sib_v, mine_p, mine_r, xg_v, perm_v, send_sem, recv_sem, l_sem,
):
    x, z, y, core, h = place()
    ck = (z % 2) * 4 + y
    up, dn, far = (y + 1) % 4, (y + 3) % 4, (y + 2) % 4
    sibling = (seq_of(x, z, y, 1 - core), h)
    x_peer = (seq_of(1 - x, z, y, core), h)
    h_peer = (seq_of(x, z, y, core), 1 - h)
    y_up = (seq_of(x, z, up, core), h)
    y_dn = (seq_of(x, z, dn, core), h)
    z_peers = [(seq_of(x, (z + d) % 8, y, core), h) for d in range(1, 8)]
    t_chips = [(ck + d) % 8 for d in range(1, 8)]
    t_peers = [(seq_of(x, (z // 2) * 2 + c // 4, c % 4, core), h) for c in t_chips]
    everyone = [sibling, x_peer, h_peer, y_up, y_dn] + z_peers + t_peers
    barrier = pltpu.get_barrier_semaphore()
    for peer in everyone:
        signal(barrier, peer)
    pl.semaphore_wait(barrier, len(everyone))
    net = Copies(send_sem, recv_sem)

    swap = net.start(wsh_ref.at[1 - core], sib_v, sibling)
    swap.wait()
    mine = wsh_ref[core] + sib_v[...]
    mine_p[...] = mine[:, :PW]
    mine_r[...] = mine[:, PW:]
    z_r = [net.start(mine_r, buf_r.at[x, z, y], peer) for peer in z_peers]
    z_p = [net.start(mine_p, buf_p.at[x, z, y], peer) for peer in z_peers]
    own_p = pltpu.make_async_copy(mine_p, buf_p.at[x, z, y], l_sem.at[0])
    own_r = pltpu.make_async_copy(mine_r, buf_r.at[x, z, y], l_sem.at[1])
    own_p.start()
    own_r.start()

    row = permuted_feature((D, 1), 0)
    col = lax.broadcasted_iota(jnp.int32, (1, D), 1)
    perm_v[...] = jnp.where(row == col, 1.0, 0.0).astype(BF)
    for i, ref in enumerate((in_ref, up_ref)):
        p = jnp.dot(ref[...].reshape(256, D), perm_v[...], preferred_element_type=F32)
        for g in range(16):
            part = jnp.concatenate([p[8 * g : 8 * g + 8], p[128 + 8 * g : 136 + 8 * g]], 0)
            xg_v[g, :, i * D : (i + 1) * D] = part.astype(BF)
    tok = [
        net.start(xg_v.at[2 * c + h], xin.at[h, ck, core], peer) for c, peer in zip(t_chips, t_peers)
    ]
    own_t = pltpu.make_async_copy(xg_v.at[2 * ck + h], xin.at[h, ck, core], l_sem.at[2])
    own_t.start()

    own_r.wait()
    for c in z_r:
        c.wait()
    r_up = net.start(buf_r.at[x, :, y], buf_r.at[x, :, y], y_up)
    r_dn = net.start(buf_r.at[x, :, y], buf_r.at[x, :, y], y_dn)
    r_x0 = net.start(buf_r.at[x, :, y], buf_r.at[x, :, y], x_peer)
    own_p.wait()
    for c in z_p:
        c.wait()
    p_x = net.start(buf_p.at[x, :, y], buf_p.at[x, :, y], x_peer)
    p_up = net.start(buf_p.at[x, :, y], buf_p.at[x, :, y], y_up)
    p_dn = net.start(buf_p.at[x, :, y], buf_p.at[x, :, y], y_dn)
    lo, hi = pl.ds(0, 4), pl.ds(4, 4)

    r_up.wait_recv()
    r_f0 = net.start(buf_r.at[x, lo, dn], buf_r.at[x, lo, dn], y_up)
    r_x1 = net.start(buf_r.at[x, :, dn], buf_r.at[x, :, dn], x_peer)
    r_dn.wait_recv()
    r_f1 = net.start(buf_r.at[x, hi, up], buf_r.at[x, hi, up], y_dn)
    r_x2 = net.start(buf_r.at[x, :, up], buf_r.at[x, :, up], x_peer)
    p_up.wait_recv()
    p_f0 = net.start(buf_p.at[x, lo, dn], buf_p.at[x, lo, dn], y_up)
    p_dn.wait_recv()
    p_f1 = net.start(buf_p.at[x, hi, up], buf_p.at[x, hi, up], y_dn)
    p_x.wait_recv()
    q_up = net.start(buf_p.at[1 - x, :, y], buf_p.at[1 - x, :, y], y_up)
    q_dn = net.start(buf_p.at[1 - x, :, y], buf_p.at[1 - x, :, y], y_dn)

    own_t.wait()
    for c in tok:
        c.wait_recv()
    t_h = net.start(xin.at[h, :, core], xin.at[h, :, core], h_peer)
    t_s = net.start(xin.at[h, :, core], xin.at[h, :, core], sibling)

    r_f0.wait_recv()
    r_x3 = net.start(buf_r.at[x, lo, far], buf_r.at[x, lo, far], x_peer)
    r_f1.wait_recv()
    r_x4 = net.start(buf_r.at[x, hi, far], buf_r.at[x, hi, far], x_peer)
    q_up.wait_recv()
    q_f0 = net.start(buf_p.at[1 - x, lo, dn], buf_p.at[1 - x, lo, dn], y_up)
    q_dn.wait_recv()
    q_f1 = net.start(buf_p.at[1 - x, hi, up], buf_p.at[1 - x, hi, up], y_dn)
    t_h.wait_recv()
    t_s2 = net.start(xin.at[1 - h, :, core], xin.at[1 - h, :, core], sibling)
    for c in (p_f0, p_f1, r_x0, r_x1, r_x2, r_x3, r_x4, q_f0, q_f1, t_s, t_s2):
        c.wait()
    for c in [r_up, r_dn, p_x, p_up, p_dn, r_f0, r_f1, q_up, q_dn, t_h] + tok:
        c.wait_send()


def normalise(v):
    mean = jnp.mean(v, -1, keepdims=True)
    centered = v - mean
    rstd = lax.rsqrt(jnp.mean(centered * centered, -1, keepdims=True) + 1e-06)
    return centered * rstd, rstd


def turn(v, by):
    return jnp.concatenate([v[:, -by:], v[:, :-by]], 1)


def nt(a, b):
    return lax.dot_general(a, b, (((1,), (1,)), ((), ())), preferred_element_type=F32)


def tn(a, b):
    return lax.dot_general(a, b, (((0,), (0,)), ((), ())), preferred_element_type=F32)


def attention(qa, ka, va, da):
    scale = HEAD_DIM ** (-0.5)
    rows = lax.broadcasted_iota(jnp.int32, (256, 256), 0)
    cols = lax.broadcasted_iota(jnp.int32, (256, 256), 1)
    same = (rows & 7) == (cols & 7)
    outs = [[[] for _ in range(3)] for _ in range(4)]
    for head, (lo, hi) in enumerate(((0, 128), (0, 256), (128, 256), (128, 384))):
        lane = lax.broadcasted_iota(jnp.int32, (1, hi - lo), 1) + lo
        keep = (lane >= HEAD_DIM * head) & (lane < HEAD_DIM * (head + 1))
        q, k, v, d = (a[:, lo:hi] for a in (qa, ka, va, da))
        qm = jnp.where(keep, q, jnp.zeros_like(q))
        dm = jnp.where(keep, d, jnp.zeros_like(d))
        scores = jnp.where(same, nt(qm, k) * scale, -1e30)
        top = jnp.max(scores, -1, keepdims=True)
        e = jnp.exp(scores - top)
        probs = e / jnp.sum(e, -1, keepdims=True)
        probs_b = probs.astype(BF)
        att = jnp.dot(probs_b, v, preferred_element_type=F32).astype(BF)
        delta = jnp.sum(dm.astype(F32) * att.astype(F32), -1, keepdims=True)
        ds = (probs * (nt(dm, v) - delta) * scale).astype(BF)
        dq = jnp.dot(ds, k, preferred_element_type=F32)
        dk = tn(ds, q)
        dv = tn(probs_b, d)
        for slot, val in zip(outs, (dq, dk, dv, att.astype(F32))):
            val = jnp.where(keep, val, 0.0)
            for t in range(lo // 128, hi // 128):
                slot[t].append(val[:, t * 128 - lo : t * 128 - lo + 128])
    return [jnp.concatenate([functools.reduce(lambda a, b: a + b, t) for t in s], 1) for s in outs]


def compute_kernel(buf_p, buf_r, xin, gate_ref, dw_p, dw_r, dn, w_v, norm_v, dz_v, g_v, f_v):
    w_v[0:1024, 0:PW] = buf_p[...].reshape(1024, PW)
    w_v[0:1024, PW:D] = buf_r[:, :, 0:RM].reshape(1024, RM)
    for r in range(2):
        f_v[...] = buf_r[:, :, RM + 128 * r : RM + 128 * (r + 1)].reshape(1024, 128).astype(F32)
        for j in range(9):
            w_v[1024 + 64 * r : 1088 + 64 * r, 128 * j : 128 * (j + 1)] = f_v[
                pl.ds(j, 64, stride=16), :
            ].astype(BF)

    lane = lax.broadcasted_iota(jnp.int32, (1, 896), 1)

    def one(pg, carry):
        tok = pl.ds(pg * 256, 256)
        src = xin[pg].reshape(256, 2 * D)
        ghat, _ = normalise(src[:, :D].astype(F32))
        normed = ghat.astype(BF)
        norm_v[tok, :] = normed
        dz = (gate_ref[...] * src[:, D:].astype(F32)).astype(BF)
        dz_v[tok, :] = dz
        qkv = jnp.dot(normed, w_v[:, 0:896], preferred_element_type=F32)
        od = jnp.dot(dz, w_v[:, 768:1152], preferred_element_type=F32)
        qa = qkv[:, 0:384].astype(BF)
        ka = turn(qkv[:, 256:640], -32).astype(BF)
        va = turn(qkv[:, 512:896], -64).astype(BF)
        da = turn(od, -96).astype(BF)
        dq, dk, dv, att = attention(qa, ka, va, da)
        dk, dv, att = turn(dk, 32), turn(dv, 64), turn(att, 96)
        tiles = [[] for _ in range(9)]
        for start, val in ((0, dq), (2, dk), (4, dv), (6, att)):
            for t in range(3):
                tiles[start + t].append(val[:, 128 * t : 128 * (t + 1)])
        for t in range(9):
            g_v[tok, 128 * t : 128 * (t + 1)] = functools.reduce(lambda a, b: a + b, tiles[t]).astype(BF)
        left = jnp.where(lane < 864, g_v[tok, 0:896], jnp.zeros((256, 896), BF))
        dn[pg] = nt(left, w_v[:, 0:896]).astype(BF)
        return carry

    lax.fori_loop(0, 2, one, 0)

    def grads(i):
        c = slice(128 * i, 128 * (i + 1))
        a = tn(norm_v[:, c], g_v[:, 0:896])
        b = tn(dz_v[:, c], g_v[:, 768:1152])
        lane = lax.broadcasted_iota(jnp.int32, (1, 128), 1)
        mid = jnp.where(lane < 96, a[:, 768:896], b[:, 0:128])
        return jnp.concatenate([a[:, 0:768], mid, b[:, 128:384]], 1)

    for i in range(8):
        block = grads(i).astype(BF).reshape(8, 16, D)
        dw_p[8 * i : 8 * i + 8] = block[:, :, :PW]
        dw_r[8 * i : 8 * i + 8, :, 0:RM] = block[:, :, PW:]
    rest = grads(8)
    for r in range(2):
        f_v[...] = jnp.zeros((1024, 128), F32)
        for j in range(9):
            f_v[pl.ds(j, 64, stride=16), :] = rest[64 * r : 64 * r + 64, 128 * j : 128 * (j + 1)]
        dw_r[:, :, RM + 128 * r : RM + 128 * (r + 1)] = f_v[...].astype(BF).reshape(64, 16, 128)


def scatter_kernel(
    dw_p, dw_r, dn, xin, gw, out,
    op, ryp, pyp, rxp, pxp, rzp, orr, rxr, pxr, ryr, pyr, rzr,
    g_v, gs_v, dn_own, rs, ps, rh, xi_v, res_v, og, perm_v, send_sem, recv_sem, l_sem,
):
    x, z, y, core, h = place()
    zl = z % 2
    ck = zl * 4 + y
    sibling = (seq_of(x, z, y, 1 - core), h)
    x_peer = (seq_of(1 - x, z, y, core), h)
    h_peer = (seq_of(x, z, y, core), 1 - h)
    z_peers = [(seq_of(x, (z + d) % 8, y, core), h) for d in range(1, 8)]
    y_peers = [(seq_of(x, z, (y + d) % 4, core), h) for d in range(1, 4)]
    base = (x * 8 + (z // 2) * 2) * 8
    member = ck * 2 + core
    group = [(base + (member + i) % 16, h) for i in range(1, 16)]
    everyone = [x_peer, h_peer] + z_peers + group
    barrier = pltpu.get_barrier_semaphore()
    for peer in everyone:
        signal(barrier, peer)
    pl.semaphore_wait(barrier, len(everyone))
    net = Copies(send_sem, recv_sem)

    away = pl.ds(pl.multiple_of((1 - core) * 128, 128), 128)
    here = pl.ds(pl.multiple_of(core * 128, 128), 128)
    swap = net.start(dn.at[:, away], rs, sibling)
    y_p = [net.start(dw_p.at[:, :, (y + d) % 4], ryp.at[d - 1], y_peers[d - 1]) for d in (1, 3, 2)]
    order = (1, 3, 2, 0)
    x_r = {d: net.start(dw_r.at[1 - x, :, (y + d) % 4], rxr.at[d], x_peer) for d in order}
    keep = pltpu.make_async_copy(dn.at[:, here], dn_own, l_sem.at[0])
    keep.start()
    keep_r = pltpu.make_async_copy(dw_r.at[x], orr, l_sem.at[1])
    keep_r.start()
    keep_p = pltpu.make_async_copy(dw_p.at[:, :, y], op, l_sem.at[2])
    keep_p.start()
    tokens = pltpu.make_async_copy(xin.at[h, pl.ds(4 * core, 4)], xi_v, l_sem.at[3])
    tokens.start()
    row = lax.broadcasted_iota(jnp.int32, (D, 1), 0)
    perm_v[...] = jnp.where(row == permuted_feature((1, D), 1), 1.0, 0.0).astype(BF)
    keep.wait()
    swap.wait_recv()
    ps[...] = (dn_own[...].astype(F32) + rs[...].astype(F32)).astype(BF)
    half = net.start(ps.at[1 - h], rh, h_peer)

    keep_r.wait()
    y_r = {}

    def x_sum(d):
        x_r[d].wait_recv()
        pxr[d] = (orr[:, (y + d) % 4].astype(F32) + rxr[d].astype(F32)).astype(BF)
        if d:
            y_r[d] = net.start(pxr.at[d], ryr.at[d - 1], y_peers[d - 1])

    x_sum(1)
    tokens.wait()
    src = xi_v[...].reshape(128, 2 * D)
    ghat, rstd = normalise(src[:, :D].astype(F32))
    half.wait_recv()
    mine = ps[h].astype(F32) + rh[...].astype(F32)
    mine = mine.astype(BF).astype(F32)
    one = jnp.mean(mine, -1, keepdims=True)
    two = jnp.mean(mine * ghat, -1, keepdims=True)
    res = src[:, D:].astype(F32) + rstd * (mine - one - ghat * two)
    res_v[...] = res.astype(BF).reshape(8, 16, D)

    local = zl == core

    def owner(i):
        to = (member + i) % 8
        return remote(
            res_v.at[to], og.at[ck, h], send_sem.at[48 + i], recv_sem.at[48 + ck],
            (base + 8 * core + to, h),
        )

    stay = pltpu.make_async_copy(res_v.at[member % 8], og.at[ck, h], l_sem.at[4])
    pl.when(jnp.logical_not(local))(lambda: owner(0).start())
    pl.when(local)(lambda: stay.start())
    for i in range(1, 8):
        owner(i).start()

    x_sum(3)
    x_sum(2)
    x_sum(0)
    keep_p.wait()
    for c in y_p:
        c.wait_recv()

    def add_y(xx):
        t = op[xx].astype(F32)
        for d in range(3):
            t = t + ryp[d, xx].astype(F32)
        pyp[xx] = t.astype(BF)

    add_y(1 - x)
    x_p = net.start(pyp.at[1 - x], rxp, x_peer)
    add_y(x)
    x_p.wait_recv()
    pxp[...] = (pyp[x].astype(F32) + rxp[...].astype(F32)).astype(BF)
    z_p = [net.start(pxp.at[(z + d) % 8], rzp.at[d - 1], z_peers[d - 1]) for d in range(1, 8)]

    pl.when(jnp.logical_not(local))(lambda: owner(0).wait_send())
    pl.when(local)(lambda: stay.wait())
    for i in range(1, 8):
        owner(i).wait_send()
    for c in range(8):
        got = remote(res_v.at[0], og.at[c, h], send_sem.at[48], recv_sem.at[48 + c], h_peer)
        pl.when(jnp.logical_not(local & (ck == c)))(lambda got=got: got.wait_recv())
    o_h = net.start(og.at[:, h], og.at[:, h], h_peer)

    for d in (1, 3, 2):
        y_r[d].wait_recv()
    t = pxr[0].astype(F32)
    for d in range(3):
        t = t + ryr[d].astype(F32)
    pyr[...] = t.astype(BF)
    z_r = [net.start(pyr.at[(z + d) % 8], rzr.at[d - 1], z_peers[d - 1]) for d in range(1, 8)]

    o_h.wait()
    back = jnp.dot(og[...].reshape(256, D), perm_v[...], preferred_element_type=F32)
    for f in range(2):
        for g in range(8):
            a = back[32 * g + 8 * f : 32 * g + 8 * f + 8]
            b = back[32 * g + 16 + 8 * f : 32 * g + 24 + 8 * f]
            out[f, 16 * g : 16 * g + 16, :] = jnp.concatenate([a, b], 0).astype(BF)

    for part, own, slots, lanes in ((z_p, pxp, rzp, (0, PW)), (z_r, pyr, rzr, (PW, BLK))):
        for c in part:
            c.wait_recv()
        t = own[z].astype(F32)
        for d in range(7):
            t = t + slots[d].astype(F32)
        g_v[:, lanes[0] : lanes[1]] = t
    last = net.start(g_v, gs_v, sibling)
    last.wait()
    gw[core] = g_v[...]
    gw[1 - core] = gs_v[...]
    for c in [swap, half, x_p] + y_p + list(x_r.values()) + list(y_r.values()) + z_p + z_r:
        c.wait_send()


def on_device(inputs, out_grad, gate, qkv_weight, out_weight):
    core = lax.axis_index("seq") % 2
    vm = pl.BlockSpec(memory_space=pltpu.VMEM)
    hbm = pl.BlockSpec(memory_space=pl.ANY)
    dma = pltpu.SemaphoreType.DMA

    w = jnp.concatenate([qkv_weight, out_weight[:, None]], 1).reshape(9, 4, 2, 288)
    w = w.transpose(2, 0, 1, 3).reshape(2, 9, D)
    main = w[:, :8]
    last = jnp.pad(w[:, 8].reshape(2, 9, 128), ((0, 0), (0, 7), (0, 0)))
    zero = jnp.zeros_like
    main = jnp.where(
        core == 0, jnp.concatenate([main, zero(main)], 1), jnp.concatenate([zero(main), main], 1)
    )
    last = jnp.where(
        core == 0, jnp.concatenate([last, zero(last)], 2), jnp.concatenate([zero(last), last], 2)
    )
    wsh = jnp.concatenate([main, last], 2)

    shape = jax.ShapeDtypeStruct
    buf_p, buf_r, xin = pl.pallas_call(
        gather_kernel,
        out_shape=[
            shape((XS, ZS, YS, 16, PW), BF), shape((XS, ZS, YS, 16, RW), BF),
            shape((2, 8, 2, 16, 2 * D), BF),
        ],
        in_specs=[vm] * 3,
        out_specs=[hbm] * 3,
        scratch_shapes=[
            pltpu.VMEM((16, BLK), BF), pltpu.VMEM((16, PW), BF), pltpu.VMEM((16, RW), BF),
            pltpu.VMEM((16, 16, 2 * D), BF), pltpu.VMEM((D, D), BF),
            dma((48,)), dma((48,)), dma((3,)),
        ],
        compiler_params=pltpu.CompilerParams(
            collective_id=0, has_side_effects=True, vmem_limit_bytes=VMEM_BYTES
        ),
        name="gather",
    )(inputs, out_grad, wsh)

    gate_p = jnp.concatenate(
        [gate.reshape(128, 9)[:, :8].reshape(1024), gate.reshape(64, 2, 9)[:, :, 8].T.reshape(128)]
    )
    dw_p, dw_r, dn = pl.pallas_call(
        compute_kernel,
        out_shape=[shape((CHIPS, 16, PW), BF), shape((CHIPS, 16, RW), BF), shape((2, 256, D), BF)],
        in_specs=[vm] * 4,
        out_specs=[vm] * 3,
        scratch_shapes=[
            pltpu.VMEM((D, D), BF), pltpu.VMEM((512, D), BF), pltpu.VMEM((512, D), BF),
            pltpu.VMEM((512, D), BF), pltpu.VMEM((1024, 128), F32),
        ],
        compiler_params=pltpu.CompilerParams(vmem_limit_bytes=VMEM_BYTES),
        name="compute",
    )(buf_p.reshape(CHIPS, 16, PW), buf_r.reshape(CHIPS, 16, RW), xin, gate_p.reshape(1, D))

    bf = lambda *dims: pltpu.VMEM(dims, BF)
    gw, grad_inputs = pl.pallas_call(
        scatter_kernel,
        out_shape=[shape((2, 16, BLK), F32), shape((2, 128, D), BF)],
        in_specs=[hbm] * 4,
        out_specs=[vm, vm],
        scratch_shapes=[
            bf(XS, ZS, 16, PW), bf(3, XS, ZS, 16, PW), bf(XS, ZS, 16, PW),
            bf(ZS, 16, PW), bf(ZS, 16, PW), bf(7, 16, PW),
            bf(ZS, YS, 16, RW), bf(YS, ZS, 16, RW), bf(YS, ZS, 16, RW),
            bf(3, ZS, 16, RW), bf(ZS, 16, RW), bf(7, 16, RW),
            pltpu.VMEM((16, BLK), F32), pltpu.VMEM((16, BLK), F32),
            bf(2, 128, D), bf(2, 128, D), bf(2, 128, D), bf(128, D), bf(4, 2, 16, 2 * D),
            bf(8, 16, D), bf(8, 2, 16, D), bf(D, D),
            dma((56,)), dma((56,)), dma((5,)),
        ],
        compiler_params=pltpu.CompilerParams(
            collective_id=1, has_side_effects=True, vmem_limit_bytes=VMEM_BYTES
        ),
        name="scatter",
    )(dw_p.reshape(XS, ZS, YS, 16, PW), dw_r.reshape(XS, ZS, YS, 16, RW), dn, xin)

    main = jnp.where(core == 0, gw[:, 0:8, :D], gw[:, 8:16, :D])
    last = jnp.where(core == 0, gw[:, 0:9, D : D + 128], gw[:, 0:9, D + 128 :]).reshape(2, 1, D)
    full = jnp.concatenate([main, last], 1).reshape(2, 9, 4, 288).transpose(1, 2, 0, 3)
    full = full.reshape(9, 4, 576)
    return grad_inputs, full[:, 0:3], full[:, 3]


def solution(mesh):
    in_specs = (
        P("seq", None, None),
        P("seq", None, None),
        P(),
        P("seq", None, "head"),
        P("seq", "head"),
    )
    out_specs = (P("seq", None, None), P("seq", None, "head"), P("seq", "head"))
    return jax.shard_map(
        on_device, mesh=mesh, in_specs=in_specs, out_specs=out_specs, check_vma=False
    )
```

```python
import functools

import jax
import jax.numpy as jnp
from jax import lax
from jax.experimental import pallas as pl
from jax.experimental.pallas import tpu as pltpu
from jax.sharding import PartitionSpec as P

D = 1152
HEAD_DIM = 72
XS, ZS, YS = 2, 8, 4
CHIPS = XS * ZS * YS
BLK = 1408
PW = 896
RW = BLK - PW
RM = D - PW
MESH = pl.DeviceIdType.MESH
BF = jnp.bfloat16
F32 = jnp.float32
VMEM_BYTES = 58 * 2**20


def place():
    s = lax.axis_index("seq")
    h = lax.axis_index("head")
    return s // 64, (s // 8) % 8, (s // 2) % 4, s % 2, h


def seq_of(x, z, y, core):
    return ((x * 8 + z) * 4 + y) * 2 + core


def signal(sem, target):
    pl.semaphore_signal(sem, inc=1, device_id=target, device_id_type=MESH)


def remote(src, dst, send, recv, target):
    return pltpu.make_async_remote_copy(
        src_ref=src, dst_ref=dst, send_sem=send, recv_sem=recv, device_id=target, device_id_type=MESH
    )


def permuted_feature(shape, dim):
    f = lax.broadcasted_iota(jnp.int32, shape, dim)
    owner = f // 9
    q = f - owner * 9
    return jnp.where(q < 8, owner * 8 + q, 1024 + (owner % 2) * 64 + owner // 2)


class Copies:
    def __init__(self, send, recv):
        self.send, self.recv, self.count = send, recv, 0

    def start(self, src, dst, target):
        k = self.count
        self.count += 1
        c = remote(src, dst, self.send.at[k], self.recv.at[k], target)
        c.start()
        return c


class RowSum:
    def __init__(self, net, src, far, got, both, up, down):
        self.net, self.src, self.far, self.got, self.both = net, src, far, got, both
        self.up, self.down = up, down

    def first(self):
        net, src = self.net, self.src
        self.f = [net.start(src(2, LO), self.far.at[0], self.up), net.start(src(2, HI), self.far.at[1], self.down)]
        self.d = [
            net.start(src(1, HI), self.got.at[0, HI], self.up),
            net.start(src(3, LO), self.got.at[1, LO], self.down),
        ]

    def second(self):
        for i, d, half, to in ((0, 1, LO, self.up), (1, 3, HI, self.down)):
            self.f[i].wait_recv()
            t = self.src(d, half)[...].astype(F32) + self.far[i].astype(F32)
            self.both[i] = t.astype(BF)
            self.d.append(self.net.start(self.both.at[i], self.got.at[i, half], to))

    def total(self):
        for c in self.d:
            c.wait_recv()
        t = self.src(0, pl.ds(0, 8))[...].astype(F32)
        return t + self.got[0].astype(F32) + self.got[1].astype(F32)

    def end(self):
        for c in self.f + self.d:
            c.wait_send()


LO, HI = pl.ds(0, 4), pl.ds(4, 4)


def normalise(v):
    mean = jnp.mean(v, -1, keepdims=True)
    centered = v - mean
    rstd = lax.rsqrt(jnp.mean(centered * centered, -1, keepdims=True) + 1e-06)
    return centered * rstd, rstd


def turn(v, by):
    return jnp.concatenate([v[:, -by:], v[:, :-by]], 1)


def nt(a, b):
    return lax.dot_general(a, b, (((1,), (1,)), ((), ())), preferred_element_type=F32)


def tn(a, b):
    return lax.dot_general(a, b, (((0,), (0,)), ((), ())), preferred_element_type=F32)


def attention(qa, ka, va, da):
    scale = HEAD_DIM ** (-0.5)
    rows = lax.broadcasted_iota(jnp.int32, (256, 256), 0)
    cols = lax.broadcasted_iota(jnp.int32, (256, 256), 1)
    same = (rows & 7) == (cols & 7)
    outs = [[[] for _ in range(3)] for _ in range(4)]
    for head, (lo, hi) in enumerate(((0, 128), (0, 256), (128, 256), (128, 384))):
        lane = lax.broadcasted_iota(jnp.int32, (1, hi - lo), 1) + lo
        keep = (lane >= HEAD_DIM * head) & (lane < HEAD_DIM * (head + 1))
        q, k, v, d = (a[:, lo:hi] for a in (qa, ka, va, da))
        qm = jnp.where(keep, q, jnp.zeros_like(q))
        dm = jnp.where(keep, d, jnp.zeros_like(d))
        scores = jnp.where(same, nt(qm, k) * scale, -1e30)
        top = jnp.max(scores, -1, keepdims=True)
        e = jnp.exp(scores - top)
        probs = e / jnp.sum(e, -1, keepdims=True)
        probs_b = probs.astype(BF)
        att = jnp.dot(probs_b, v, preferred_element_type=F32).astype(BF)
        delta = jnp.sum(dm.astype(F32) * att.astype(F32), -1, keepdims=True)
        ds = (probs * (nt(dm, v) - delta) * scale).astype(BF)
        dq = jnp.dot(ds, k, preferred_element_type=F32)
        dk = tn(ds, q)
        dv = tn(probs_b, d)
        for slot, val in zip(outs, (dq, dk, dv, att.astype(F32))):
            val = jnp.where(keep, val, 0.0)
            for t in range(lo // 128, hi // 128):
                slot[t].append(val[:, t * 128 - lo : t * 128 - lo + 128])
    return [jnp.concatenate([functools.reduce(lambda a, b: a + b, t) for t in s], 1) for s in outs]


def kernel(
    in_ref, up_ref, gate_ref, wq_ref, wo_ref, out, gq, go,
    sib_v, away_v, mine_p, mine_r, nat_v, xg_v, perm_v, rstd_v, buf_p, buf_r, xin,
    w_v, g_v, f_v, dw_p, dw_r, dn, rs, ps, rh, res_v, og,
    far_p, got_p, both_p, pyp, rxp, pxp, rzp, rxr, pxr, far_r, got_r, both_r, pyr, rzr, fin_v, fsib_v,
    send_sem, recv_sem, o_send, o_recv, s_send, s_recv, l_sem,
):
    x, z, y, core, h = place()
    zl = z % 2
    ck = zl * 4 + y
    member = ck * 2 + core
    base = (x * 8 + (z // 2) * 2) * 8
    above, below, far = (y + 1) % 4, (y + 3) % 4, (y + 2) % 4
    sibling = (seq_of(x, z, y, 1 - core), h)
    x_peer = (seq_of(1 - x, z, y, core), h)
    h_peer = (seq_of(x, z, y, core), 1 - h)
    y_up = (seq_of(x, z, above, core), h)
    y_dn = (seq_of(x, z, below, core), h)
    z_peers = [(seq_of(x, (z + d) % 8, y, core), h) for d in range(1, 8)]
    t_chips = [(ck + d) % 8 for d in range(1, 8)]
    t_peers = [(seq_of(x, (z // 2) * 2 + c // 4, c % 4, core), h) for c in t_chips]
    group = [(base + (member + i) % 16, h) for i in range(1, 16)]
    everyone = [x_peer, h_peer] + z_peers + group
    barrier = pltpu.get_barrier_semaphore()
    for peer in everyone:
        signal(barrier, peer)

    wq, wo = wq_ref[...].astype(F32), wo_ref[...].astype(F32)
    blocks = []
    for half in range(2):
        c = slice(288 * half, 288 * half + 288)
        rows = jnp.concatenate([wq[:, 0, c], wq[:, 1, c], wq[:, 2, c], wo[:, c]], 1)
        main, last = rows[0:8], rows[8:9]
        last = [last[:, 128 * j : 128 * j + 128] for j in range(9)] + [jnp.zeros((7, 128), F32)]
        last = jnp.concatenate(last, 0)
        main0 = jnp.concatenate([main, jnp.zeros((8, D), F32)], 0)
        main1 = jnp.concatenate([jnp.zeros((8, D), F32), main], 0)
        none = jnp.zeros((16, 128), F32)
        block0 = jnp.concatenate([main0, last, none], 1)
        block1 = jnp.concatenate([main1, none, last], 1)
        blocks.append(jnp.where(core == 0, block0, block1))
    away_v[...] = jnp.where(core == 0, blocks[1], blocks[0]).astype(BF)
    mine = jnp.where(core == 0, blocks[0], blocks[1])
    pl.semaphore_wait(barrier, len(everyone))
    net = Copies(send_sem, recv_sem)

    swap = net.start(away_v, sib_v, sibling)
    row = permuted_feature((D, 1), 0)
    col = lax.broadcasted_iota(jnp.int32, (1, D), 1)
    perm_v[...] = jnp.where(row == col, 1.0, 0.0).astype(BF)
    swap.wait()
    mine = (mine + sib_v[...].astype(F32)).astype(BF)
    mine_p[...] = mine[:, :PW]
    mine_r[...] = mine[:, PW:]
    z_r = [net.start(mine_r, buf_r.at[x, z, y], peer) for peer in z_peers]
    z_p = [net.start(mine_p, buf_p.at[x, z, y], peer) for peer in z_peers]
    buf_p[x, z, y] = mine[:, :PW]
    buf_r[x, z, y] = mine[:, PW:]

    ghat, rstd = normalise(in_ref[...].reshape(256, D).astype(F32))
    rstd_v[...] = rstd
    dz = gate_ref[...] * up_ref[...].reshape(256, D).astype(F32)
    for i, val in enumerate((ghat, dz)):
        nat_v[...] = val.astype(BF)
        p = jnp.dot(nat_v[...], perm_v[...], preferred_element_type=F32)
        for g in range(16):
            part = jnp.concatenate([p[8 * g : 8 * g + 8], p[128 + 8 * g : 136 + 8 * g]], 0)
            xg_v[g, :, i * D : (i + 1) * D] = part.astype(BF)
    tok = [
        net.start(xg_v.at[2 * c + h], xin.at[h, ck, core], peer) for c, peer in zip(t_chips, t_peers)
    ]
    own_t = pltpu.make_async_copy(xg_v.at[2 * ck + h], xin.at[h, ck, core], l_sem.at[0])
    own_t.start()

    for c in z_r:
        c.wait()
    r_up = net.start(buf_r.at[x, :, y], buf_r.at[x, :, y], y_up)
    r_dn = net.start(buf_r.at[x, :, y], buf_r.at[x, :, y], y_dn)
    r_x0 = net.start(buf_r.at[x, :, y], buf_r.at[x, :, y], x_peer)
    for c in z_p:
        c.wait()
    p_x = net.start(buf_p.at[x, :, y], buf_p.at[x, :, y], x_peer)
    p_up = net.start(buf_p.at[x, :, y], buf_p.at[x, :, y], y_up)
    p_dn = net.start(buf_p.at[x, :, y], buf_p.at[x, :, y], y_dn)

    r_up.wait_recv()
    r_f0 = net.start(buf_r.at[x, LO, below], buf_r.at[x, LO, below], y_up)
    r_x1 = net.start(buf_r.at[x, :, below], buf_r.at[x, :, below], x_peer)
    r_dn.wait_recv()
    r_f1 = net.start(buf_r.at[x, HI, above], buf_r.at[x, HI, above], y_dn)
    r_x2 = net.start(buf_r.at[x, :, above], buf_r.at[x, :, above], x_peer)
    p_up.wait_recv()
    p_f0 = net.start(buf_p.at[x, LO, below], buf_p.at[x, LO, below], y_up)
    p_dn.wait_recv()
    p_f1 = net.start(buf_p.at[x, HI, above], buf_p.at[x, HI, above], y_dn)
    p_x.wait_recv()
    q_up = net.start(buf_p.at[1 - x, :, y], buf_p.at[1 - x, :, y], y_up)
    q_dn = net.start(buf_p.at[1 - x, :, y], buf_p.at[1 - x, :, y], y_dn)

    own_t.wait()
    for c in tok:
        c.wait_recv()
    t_h = net.start(xin.at[h, :, core], xin.at[h, :, core], h_peer)
    t_s = net.start(xin.at[h, :, core], xin.at[h, :, core], sibling)

    r_f0.wait_recv()
    r_x3 = net.start(buf_r.at[x, LO, far], buf_r.at[x, LO, far], x_peer)
    r_f1.wait_recv()
    r_x4 = net.start(buf_r.at[x, HI, far], buf_r.at[x, HI, far], x_peer)
    q_up.wait_recv()
    q_f0 = net.start(buf_p.at[1 - x, LO, below], buf_p.at[1 - x, LO, below], y_up)
    q_dn.wait_recv()
    q_f1 = net.start(buf_p.at[1 - x, HI, above], buf_p.at[1 - x, HI, above], y_dn)
    t_h.wait_recv()
    t_s2 = net.start(xin.at[1 - h, :, core], xin.at[1 - h, :, core], sibling)
    for c in (p_f0, p_f1, r_x0, r_x1, r_x2, r_x3, r_x4, q_f0, q_f1, t_s, t_s2):
        c.wait()
    for c in [r_up, r_dn, p_x, p_up, p_dn, r_f0, r_f1, q_up, q_dn, t_h] + tok:
        c.wait_send()

    w_v[0:1024, 0:PW] = buf_p[...].reshape(1024, PW)
    w_v[0:1024, PW:D] = buf_r[:, :, :, :, 0:RM].reshape(1024, RM)
    for r in range(2):
        f_v[...] = buf_r[:, :, :, :, RM + 128 * r : RM + 128 * (r + 1)].reshape(1024, 128).astype(F32)
        for j in range(9):
            w_v[1024 + 64 * r : 1088 + 64 * r, 128 * j : 128 * (j + 1)] = f_v[
                pl.ds(j, 64, stride=16), :
            ].astype(BF)

    lane = lax.broadcasted_iota(jnp.int32, (1, 896), 1)
    away = pl.ds(pl.multiple_of((1 - core) * 128, 128), 128)
    here = pl.ds(pl.multiple_of(core * 128, 128), 128)

    def swap_dn(pg):
        return remote(dn.at[pg, away], rs.at[pg], s_send.at[pg], s_recv.at[pg], sibling)

    def tokens(pg, carry):
        tok = pl.ds(pg * 256, 256)
        src = xin[pg].reshape(256, 2 * D)
        qkv = jnp.dot(src[:, :D], w_v[:, 0:896], preferred_element_type=F32)
        od = jnp.dot(src[:, D:], w_v[:, 768:1152], preferred_element_type=F32)
        qa = qkv[:, 0:384].astype(BF)
        ka = turn(qkv[:, 256:640], -32).astype(BF)
        va = turn(qkv[:, 512:896], -64).astype(BF)
        da = turn(od, -96).astype(BF)
        dq, dk, dv, att = attention(qa, ka, va, da)
        dk, dv, att = turn(dk, 32), turn(dv, 64), turn(att, 96)
        tiles = [[] for _ in range(9)]
        for start, val in ((0, dq), (2, dk), (4, dv), (6, att)):
            for t in range(3):
                tiles[start + t].append(val[:, 128 * t : 128 * (t + 1)])
        for t in range(9):
            g_v[tok, 128 * t : 128 * (t + 1)] = functools.reduce(lambda a, b: a + b, tiles[t]).astype(BF)
        left = jnp.where(lane < 864, g_v[tok, 0:896], jnp.zeros((256, 896), BF))
        dn[pg] = nt(left, w_v[:, 0:896]).astype(BF)
        swap_dn(pg).start()
        return carry

    lax.fori_loop(0, 2, tokens, 0)

    def grads(i):
        a = tn(xin[:, :, :, :, pl.ds(pl.multiple_of(128 * i, 128), 128)].reshape(512, 128), g_v[:, 0:896])
        b = tn(
            xin[:, :, :, :, pl.ds(pl.multiple_of(D + 128 * i, 128), 128)].reshape(512, 128),
            g_v[:, 768:1152],
        )
        lane = lax.broadcasted_iota(jnp.int32, (1, 128), 1)
        mid = jnp.where(lane < 96, a[:, 768:896], b[:, 0:128])
        return jnp.concatenate([a[:, 0:768], mid, b[:, 128:384]], 1)

    def grad_rows(xx):
        def body(j, carry):
            block = grads(4 * xx + j).astype(BF).reshape(2, 4, 16, D)
            dw_p[xx, pl.ds(2 * j, 2)] = block[:, :, :, :PW]
            dw_r[xx, pl.ds(2 * j, 2), :, :, 0:RM] = block[:, :, :, PW:]
            return carry

        lax.fori_loop(0, 4, body, 0)

    rest = grads(8)
    for r in range(2):
        f_v[...] = jnp.zeros((1024, 128), F32)
        for j in range(9):
            f_v[pl.ds(j, 64, stride=16), :] = rest[64 * r : 64 * r + 64, 128 * j : 128 * (j + 1)]
        dw_r[:, :, :, :, RM + 128 * r : RM + 128 * (r + 1)] = f_v[...].astype(BF).reshape(2, 8, 4, 16, 128)
    grad_rows(1 - x)

    x_r = {d: net.start(dw_r.at[1 - x, :, (y + d) % 4], rxr.at[d], x_peer) for d in (2, 1, 3, 0)}
    sums = [
        RowSum(
            net, (lambda d, zs, xx=xx: dw_p.at[xx, zs, (y + d) % 4]),
            far_p.at[i], got_p.at[i], both_p.at[i], y_up, y_dn,
        )
        for i, xx in enumerate((1 - x, x))
    ]
    sum_r = RowSum(net, (lambda d, zs: pxr.at[d, zs]), far_r, got_r, both_r, y_up, y_dn)
    sums[0].first()
    for pg in range(2):
        swap_dn(pg).wait_recv()
    ps[...] = (dn[:, here].astype(F32) + rs[...].astype(F32)).astype(BF)
    dn_h = net.start(ps.at[1 - h], rh, h_peer)
    grad_rows(x)
    sums[1].first()
    sums[0].second()

    def x_sum(d):
        x_r[d].wait_recv()
        pxr[d] = (dw_r[x, :, (y + d) % 4].astype(F32) + rxr[d].astype(F32)).astype(BF)

    x_sum(2)
    x_sum(1)
    x_sum(3)
    sum_r.first()
    sums[1].second()

    dn_h.wait_recv()
    mine = ps[h].astype(F32) + rh[...].astype(F32)
    mine = mine.astype(BF).astype(F32)
    ghat = xin[h, pl.ds(4 * core, 4), :, :, 0:D].reshape(128, D).astype(F32)
    one = jnp.mean(mine, -1, keepdims=True)
    two = jnp.mean(mine * ghat, -1, keepdims=True)
    res_v[...] = (mine - one - ghat * two).astype(BF).reshape(8, 16, D)

    local = zl == core

    def owner(i):
        to = (member + i) % 8
        target = (base + 8 * core + to, h)
        return remote(res_v.at[to], og.at[ck, h], o_send.at[i], o_recv.at[ck], target)

    stay = pltpu.make_async_copy(res_v.at[member % 8], og.at[ck, h], l_sem.at[1])
    pl.when(jnp.logical_not(local))(lambda: owner(0).start())
    pl.when(local)(lambda: stay.start())
    for i in range(1, 8):
        owner(i).start()

    x_sum(0)
    pyp[0] = sums[0].total().astype(BF)
    x_p = net.start(pyp.at[0], rxp, x_peer)
    sum_r.second()
    pyp[1] = sums[1].total().astype(BF)
    x_p.wait_recv()
    pxp[...] = (pyp[1].astype(F32) + rxp[...].astype(F32)).astype(BF)
    z_p = [net.start(pxp.at[(z + d) % 8], rzp.at[d - 1], z_peers[d - 1]) for d in range(1, 8)]

    pl.when(jnp.logical_not(local))(lambda: owner(0).wait_send())
    pl.when(local)(lambda: stay.wait())
    for i in range(1, 8):
        owner(i).wait_send()
    for c in range(8):
        got = remote(res_v.at[0], og.at[c, h], o_send.at[0], o_recv.at[c], h_peer)
        pl.when(jnp.logical_not(local & (ck == c)))(lambda got=got: got.wait_recv())
    o_h = net.start(og.at[:, h], og.at[:, h], h_peer)

    pyr[...] = sum_r.total().astype(BF)
    z_r = [net.start(pyr.at[(z + d) % 8], rzr.at[d - 1], z_peers[d - 1]) for d in range(1, 8)]

    o_h.wait()
    back = nt(og[...].reshape(256, D), perm_v[...])
    for f in range(2):
        nat = jnp.concatenate([back[16 * g + 8 * f : 16 * g + 8 * f + 8] for g in range(16)], 0)
        nat = up_ref[f].astype(F32) + rstd_v[128 * f : 128 * f + 128] * nat
        out[f] = nat.astype(BF)

    for part, own, slots, lanes in ((z_p, pxp, rzp, (0, PW)), (z_r, pyr, rzr, (PW, BLK))):
        for c in part:
            c.wait_recv()
        t = own[z].astype(F32)
        for d in range(7):
            t = t + slots[d].astype(F32)
        fin_v[:, lanes[0] : lanes[1]] = t
    last = net.start(fin_v, fsib_v, sibling)
    last.wait()

    mine, other = fin_v[...], fsib_v[...]
    rows = []
    for half in (jnp.where(core == 0, mine, other), jnp.where(core == 0, other, mine)):
        main = jnp.where(core == 0, half[0:8, :D], half[8:16, :D])
        tail = jnp.where(core == 0, half[0:9, D : D + 128], half[0:9, D + 128 :])
        tail = jnp.concatenate([tail[j : j + 1] for j in range(9)], 1)
        rows.append(jnp.concatenate([main, tail], 0))
    for t in range(4):
        both = jnp.concatenate([r[:, 288 * t : 288 * t + 288] for r in rows], 1)
        if t < 3:
            gq[:, t, :] = both
        else:
            go[...] = both

    for pg in range(2):
        swap_dn(pg).wait_send()
    for c in [dn_h, x_p] + list(x_r.values()) + z_p + z_r:
        c.wait_send()
    for s in sums + [sum_r]:
        s.end()


def on_device(inputs, out_grad, gate, qkv_weight, out_weight):
    vm = pl.BlockSpec(memory_space=pltpu.VMEM)
    dma = pltpu.SemaphoreType.DMA
    shape = jax.ShapeDtypeStruct
    bf = lambda *dims: pltpu.VMEM(dims, BF)
    f32 = lambda *dims: pltpu.VMEM(dims, F32)
    grad_inputs, grad_qkv, grad_out = pl.pallas_call(
        kernel,
        out_shape=[shape((2, 128, D), BF), shape((9, 3, 576), F32), shape((9, 576), F32)],
        in_specs=[vm] * 5,
        out_specs=[vm] * 3,
        scratch_shapes=[
            bf(16, BLK), bf(16, BLK), bf(16, PW), bf(16, RW), bf(256, D), bf(16, 16, 2 * D), bf(D, D),
            f32(256, 1), bf(XS, ZS, YS, 16, PW), bf(XS, ZS, YS, 16, RW), bf(2, 8, 2, 16, 2 * D),
            bf(D, D), bf(512, D), f32(1024, 128), bf(XS, ZS, YS, 16, PW), bf(XS, ZS, YS, 16, RW),
            bf(2, 256, D), bf(2, 128, D), bf(2, 128, D), bf(128, D), bf(8, 16, D), bf(8, 2, 16, D),
            bf(2, 2, 4, 16, PW), bf(2, 2, ZS, 16, PW), bf(2, 2, 4, 16, PW), bf(2, ZS, 16, PW),
            bf(ZS, 16, PW), bf(ZS, 16, PW), bf(7, 16, PW),
            bf(YS, ZS, 16, RW), bf(YS, ZS, 16, RW), bf(2, 4, 16, RW), bf(2, ZS, 16, RW),
            bf(2, 4, 16, RW), bf(ZS, 16, RW), bf(7, 16, RW), f32(16, BLK), f32(16, BLK),
            dma((88,)), dma((88,)), dma((8,)), dma((8,)), dma((2,)), dma((2,)), dma((2,)),
        ],
        compiler_params=pltpu.CompilerParams(
            collective_id=0, has_side_effects=True, vmem_limit_bytes=VMEM_BYTES
        ),
        name="sublayer_backward",
    )(inputs, out_grad, gate.reshape(1, D), qkv_weight, out_weight)
    return grad_inputs, grad_qkv, grad_out


def solution(mesh):
    in_specs = (
        P("seq", None, None),
        P("seq", None, None),
        P(),
        P("seq", None, "head"),
        P("seq", "head"),
    )
    out_specs = (P("seq", None, None), P("seq", None, "head"), P("seq", "head"))
    return jax.shard_map(
        on_device, mesh=mesh, in_specs=in_specs, out_specs=out_specs, check_vma=False
    )
```

```python
import functools

import jax
import jax.numpy as jnp
from jax import lax
from jax.experimental import pallas as pl
from jax.experimental.pallas import tpu as pltpu
from jax.sharding import PartitionSpec as P

D = 1152
HEAD_DIM = 72
XS, ZS, YS = 2, 8, 4
CHIPS = XS * ZS * YS
BLK = 1408
GP, SP = 512, 640
GW, SW = GP + BLK - D, SP + BLK - D
GQ, SQ = D - GP, D - SP
OFFS = (0, 7, 1, 6, 2, 5, 3, 4)
SLOT = tuple(OFFS.index(d) for d in range(8))
GROUPS = (pl.ds(0, 1), pl.ds(1, 2), pl.ds(3, 2), pl.ds(5, 3))
MESH = pl.DeviceIdType.MESH
BF = jnp.bfloat16
F32 = jnp.float32
VMEM_BYTES = 58 * 2**20


def place():
    s = lax.axis_index("seq")
    h = lax.axis_index("head")
    return s // 64, (s // 8) % 8, (s // 2) % 4, s % 2, h


def seq_of(x, z, y, core):
    return ((x * 8 + z) * 4 + y) * 2 + core


def signal(sem, target):
    pl.semaphore_signal(sem, inc=1, device_id=target, device_id_type=MESH)


def remote(src, dst, send, recv, target):
    return pltpu.make_async_remote_copy(
        src_ref=src, dst_ref=dst, send_sem=send, recv_sem=recv, device_id=target, device_id_type=MESH
    )


def permuted_feature(shape, dim):
    f = lax.broadcasted_iota(jnp.int32, shape, dim)
    owner = f // 9
    q = f - owner * 9
    return jnp.where(q < 8, owner * 8 + q, 1024 + (owner % 2) * 64 + owner // 2)


class Copies:
    def __init__(self, send, recv):
        self.send, self.recv, self.count = send, recv, 0

    def start(self, src, dst, target):
        k = self.count
        self.count += 1
        c = remote(src, dst, self.send.at[k], self.recv.at[k], target)
        c.start()
        return c


class RowSum:
    def __init__(self, net, src, far, got, both, up, down, by_up):
        self.net, self.src, self.far, self.got, self.both = net, src, far, got, both
        self.up, self.down, self.by_up = up, down, by_up

    def first(self):
        net, src = self.net, self.src
        if self.by_up:
            self.c = [net.start(src(2), self.far, self.up), net.start(src(3), self.got[1], self.down)]
        else:
            self.c = [net.start(src(2), self.far, self.down), net.start(src(1), self.got[0], self.up)]

    def second(self):
        self.c[0].wait_recv()
        t = self.src(1 if self.by_up else 3)[...].astype(F32) + self.far[...].astype(F32)
        self.both[...] = t.astype(BF)
        if self.by_up:
            self.c.append(self.net.start(self.both, self.got[0], self.up))
        else:
            self.c.append(self.net.start(self.both, self.got[1], self.down))

    def total(self):
        self.c[1].wait_recv()
        self.c[2].wait_recv()
        t = self.src(0)[...].astype(F32)
        return t + self.got[0][...].astype(F32) + self.got[1][...].astype(F32)

    def end(self):
        for c in self.c:
            c.wait_send()


def normalise(v):
    mean = jnp.mean(v, -1, keepdims=True)
    centered = v - mean
    rstd = lax.rsqrt(jnp.mean(centered * centered, -1, keepdims=True) + 1e-06)
    return centered * rstd, rstd


def turn(v, by):
    return jnp.concatenate([v[:, -by:], v[:, :-by]], 1)


def nt(a, b):
    return lax.dot_general(a, b, (((1,), (1,)), ((), ())), preferred_element_type=F32)


def tn(a, b):
    return lax.dot_general(a, b, (((0,), (0,)), ((), ())), preferred_element_type=F32)


def attention(qa, ka, va, da):
    scale = HEAD_DIM ** (-0.5)
    rows = lax.broadcasted_iota(jnp.int32, (256, 256), 0)
    cols = lax.broadcasted_iota(jnp.int32, (256, 256), 1)
    same = (rows & 7) == (cols & 7)
    outs = [[[] for _ in range(3)] for _ in range(4)]
    for head, (lo, hi) in enumerate(((0, 128), (0, 256), (128, 256), (128, 384))):
        lane = lax.broadcasted_iota(jnp.int32, (1, hi - lo), 1) + lo
        keep = (lane >= HEAD_DIM * head) & (lane < HEAD_DIM * (head + 1))
        q, k, v, d = (a[:, lo:hi] for a in (qa, ka, va, da))
        qm = jnp.where(keep, q, jnp.zeros_like(q))
        dm = jnp.where(keep, d, jnp.zeros_like(d))
        scores = jnp.where(same, nt(qm, k) * scale, -1e30)
        top = jnp.max(scores, -1, keepdims=True)
        e = jnp.exp(scores - top)
        probs = e / jnp.sum(e, -1, keepdims=True)
        probs_b = probs.astype(BF)
        att = jnp.dot(probs_b, v, preferred_element_type=F32).astype(BF)
        delta = jnp.sum(dm.astype(F32) * att.astype(F32), -1, keepdims=True)
        ds = (probs * (nt(dm, v) - delta) * scale).astype(BF)
        dq = jnp.dot(ds, k, preferred_element_type=F32)
        dk = tn(ds, q)
        dv = tn(probs_b, d)
        for slot, val in zip(outs, (dq, dk, dv, att.astype(F32))):
            val = jnp.where(keep, val, 0.0)
            for t in range(lo // 128, hi // 128):
                slot[t].append(val[:, t * 128 - lo : t * 128 - lo + 128])
    return [jnp.concatenate([functools.reduce(lambda a, b: a + b, t) for t in s], 1) for s in outs]


def kernel(
    in_hbm, up_hbm, gate_ref, wq_ref, wo_ref, out, gq, go,
    in_ref, up_ref, sib_v, away_v, mine_p, mine_q, nat_v, xg_v, perm_v, rstd_v, buf_p, buf_q, xin,
    w_v, g_v, f_v, dw_p, dw_q, dn, rs, ps, rh, res_v, og,
    far_p, got_p, both_p, pyp, rxp, pxp, rzp, rq, tq, zq, far_q, got_q, both_q, pq, rxq, fin_v, fsib_v,
    send_sem, recv_sem, o_send, o_recv, s_send, s_recv, l_sem,
):
    x, z, y, core, h = place()
    zl = z % 2
    ck = zl * 4 + y
    member = ck * 2 + core
    base = (x * 8 + (z // 2) * 2) * 8
    above, below, far = (y + 1) % 4, (y + 3) % 4, (y + 2) % 4
    sibling = (seq_of(x, z, y, 1 - core), h)
    x_peer = (seq_of(1 - x, z, y, core), h)
    h_peer = (seq_of(x, z, y, core), 1 - h)
    y_up = (seq_of(x, z, above, core), h)
    y_dn = (seq_of(x, z, below, core), h)
    z_up = (seq_of(x, (z + 1) % 8, y, core), h)
    z_dn = (seq_of(x, (z + 7) % 8, y, core), h)
    z_peers = [(seq_of(x, (z + d) % 8, y, core), h) for d in range(1, 8)]
    plane, other = pl.ds(zl * 4, 4), pl.ds((1 - zl) * 4, 4)
    zb = (z // 2) * 2
    near_peers = [(seq_of(x, z, yy, core), h) for yy in [(y + d) % 4 for d in range(1, 4)]]
    cross_peers = [(seq_of(x, zb + 1 - zl, yy, core), h) for yy in [(y + d) % 4 for d in range(4)]]
    group = [(base + (member + i) % 16, h) for i in range(1, 16)]
    everyone = [x_peer, h_peer] + z_peers + group
    net = Copies(send_sem, recv_sem)
    barrier = pltpu.get_barrier_semaphore()
    for peer in everyone:
        signal(barrier, peer)

    load = [
        pltpu.make_async_copy(in_hbm, in_ref, l_sem.at[2]),
        pltpu.make_async_copy(up_hbm, up_ref, l_sem.at[3]),
    ]
    for c in load:
        c.start()

    wq, wo = wq_ref[...].astype(F32), wo_ref[...].astype(F32)
    blocks = []
    for half in range(2):
        c = slice(288 * half, 288 * half + 288)
        rows = jnp.concatenate([wq[:, 0, c], wq[:, 1, c], wq[:, 2, c], wo[:, c]], 1)
        main, last = rows[0:8], rows[8:9]
        last = [last[:, 128 * j : 128 * j + 128] for j in range(9)] + [jnp.zeros((7, 128), F32)]
        last = jnp.concatenate(last, 0)
        main0 = jnp.concatenate([main, jnp.zeros((8, D), F32)], 0)
        main1 = jnp.concatenate([jnp.zeros((8, D), F32), main], 0)
        none = jnp.zeros((16, 128), F32)
        block0 = jnp.concatenate([main0, last, none], 1)
        block1 = jnp.concatenate([main1, none, last], 1)
        blocks.append(jnp.where(core == 0, block0, block1))
    away_v[...] = jnp.where(core == 0, blocks[1], blocks[0]).astype(BF)
    mine = jnp.where(core == 0, blocks[0], blocks[1])
    row = permuted_feature((D, 1), 0)
    col = lax.broadcasted_iota(jnp.int32, (1, D), 1)
    perm_v[...] = jnp.where(row == col, 1.0, 0.0).astype(BF)
    for c in load:
        c.wait()
    ghat, rstd = normalise(in_ref[...].reshape(256, D).astype(F32))
    rstd_v[...] = rstd
    nat_v[0] = ghat.astype(BF)
    nat_v[1] = (gate_ref[...].reshape(1, D) * up_ref[...].reshape(256, D).astype(F32)).astype(BF)
    pl.semaphore_wait(barrier, len(everyone))

    swap = net.start(away_v, sib_v, sibling)
    for i in range(2):
        p = jnp.dot(nat_v[i], perm_v[...], preferred_element_type=F32)
        for g in range(16):
            part = jnp.concatenate([p[8 * g : 8 * g + 8], p[128 + 8 * g : 136 + 8 * g]], 0)
            xg_v[g, :, i * D : (i + 1) * D] = part.astype(BF)
    swap.wait()
    mine = (mine + sib_v[...].astype(F32)).astype(BF)
    own_q = mine[:, GP:D]
    mine_p[:, 0:GP] = mine[:, :GP]
    mine_p[:, GP:GW] = mine[:, D:]
    mine_q[...] = own_q
    buf_p[x, 0, y, :, 0:GP] = mine[:, :GP]
    buf_p[x, 0, y, :, GP:GW] = mine[:, D:]
    buf_q[z, x, y] = own_q
    q_x = net.start(mine_q, buf_q.at[z, x, y], x_peer)
    sent = [{} for _ in GROUPS]

    def first(g):
        own = buf_p.at[x, GROUPS[g], y]
        for way, peer in (("up", y_up), ("dn", y_dn), ("x", x_peer)):
            sent[g][way] = net.start(own, own, peer)

    z_c = {}

    def z_send(d):
        z_c[d] = net.start(mine_p, buf_p.at[x, SLOT[8 - d], y], z_peers[d - 1])

    def arrived(g):
        for j in range(GROUPS[g].start, GROUPS[g].start + GROUPS[g].size):
            z_c[8 - OFFS[j]].wait_recv()

    def second(g):
        t = sent[g]
        t["up"].wait_recv()
        got = buf_p.at[x, GROUPS[g], below]
        t["f"] = net.start(got, got, y_up)
        t["x"].wait_recv()
        own = buf_p.at[1 - x, GROUPS[g], y]
        t["oup"] = net.start(own, own, y_up)
        t["odn"] = net.start(own, own, y_dn)

    def third(g):
        t = sent[g]
        t["odn"].wait_recv()
        got = buf_p.at[1 - x, GROUPS[g], above]
        t["of"] = net.start(got, got, y_dn)

    def pass_on(at, peer):
        return net.start(at, at, peer)

    tok, tok_z = {}, {}

    def tok_near(d):
        to = zl * 4 + (y + d) % 4
        tok[d] = net.start(xg_v.at[pl.ds(2 * to, 2)], xin.at[:, ck, core], near_peers[d - 1])

    def tok_cross(d):
        to = (1 - zl) * 4 + (y + d) % 4
        tok_z[d] = net.start(xg_v.at[2 * to + h], xin.at[h, ck, core], cross_peers[d])

    t_h = []

    def tok_share(d):
        tok_z[d].wait_recv()
        t_h.append(pass_on(xin.at[h, (1 - zl) * 4 + (y + 4 - d) % 4, core], h_peer))

    for d in (1, 7, 2, 6, 3, 5, 4):
        z_send(d)
    first(0)
    own_t = pltpu.make_async_copy(xg_v.at[pl.ds(2 * ck, 2)], xin.at[:, ck, core], l_sem.at[0])
    own_t.start()
    q_x.wait_recv()
    q_c = [pass_on(buf_q.at[z, :, y], y_up), pass_on(buf_q.at[z, :, y], y_dn)]
    arrived(1)
    first(1)
    q_c[0].wait_recv()
    q_f0 = pass_on(buf_q.at[z, 0, below], y_up)
    q_c[1].wait_recv()
    q_f1 = pass_on(buf_q.at[z, 1, above], y_dn)
    tok_cross(0)
    tok_cross(2)
    arrived(2)
    first(2)
    second(0)
    q_f0.wait_recv()
    q_f1.wait_recv()
    ring_up, ring_dn = [[], []], [[], []]
    for i in range(2):
        ring_up[i].append(pass_on(buf_q.at[z, i], z_up))
        ring_dn[i].append(pass_on(buf_q.at[z, i], z_dn))

    def ring(step):
        for i in range(2):
            ring_up[i][-1].wait_recv()
            if step < 3 or i == 0:
                ring_up[i].append(pass_on(buf_q.at[(z + 8 - step) % 8, i], z_up))
            ring_dn[i][-1].wait_recv()
            if step < 3 or i == 1:
                ring_dn[i].append(pass_on(buf_q.at[(z + step) % 8, i], z_dn))

    tok_cross(1)
    arrived(3)
    first(3)
    second(1)
    tok_near(1)
    tok_near(3)
    tok_share(0)
    tok_share(2)
    ring(1)
    tok_cross(3)
    third(0)
    second(2)
    third(1)
    tok_share(1)
    ring(2)
    second(3)
    tok_near(2)
    third(2)
    ring(3)
    tok_share(3)
    third(3)
    own_t.wait()
    for d in (1, 3, 2):
        tok[d].wait_recv()
    t_s = [pass_on(xin.at[:, plane, core], sibling)]
    for c in t_h:
        c.wait_recv()
    t_s.append(pass_on(xin.at[:, other, core], sibling))
    ring_up[0][-1].wait_recv()
    ring_dn[1][-1].wait_recv()
    for g, t in enumerate(sent):
        for name in ("dn", "f", "of", "oup"):
            t[name].wait_recv()
    for c in t_s:
        c.wait_recv()

    for xx in range(2):
        for j in range(8):
            k = pl.ds(pl.multiple_of((xx * 8 + (z + OFFS[j]) % 8) * 64, 64), 64)
            w_v[k, 0:GP] = buf_p[xx, j, :, :, 0:GP].reshape(64, GP)
        for zz in range(8):
            k = (xx * 8 + zz) * 64
            w_v[k : k + 64, GP:D] = buf_q[zz, xx].reshape(64, GQ)
    for r in range(2):
        for xx in range(2):
            for j in range(8):
                k = pl.ds(pl.multiple_of((xx * 8 + (z + OFFS[j]) % 8) * 64, 64), 64)
                part = buf_p[xx, j, :, :, GP + 128 * r : GP + 128 * (r + 1)]
                f_v[k, :] = part.reshape(64, 128).astype(F32)
        for j in range(9):
            w_v[1024 + 64 * r : 1088 + 64 * r, 128 * j : 128 * (j + 1)] = f_v[
                pl.ds(j, 64, stride=16), :
            ].astype(BF)

    lane = lax.broadcasted_iota(jnp.int32, (1, 896), 1)
    away = pl.ds(pl.multiple_of((1 - core) * 128, 128), 128)
    here = pl.ds(pl.multiple_of(core * 128, 128), 128)

    def swap_dn(pg):
        return remote(dn.at[pg, away], rs.at[pg], s_send.at[pg], s_recv.at[pg], sibling)

    def tokens(pg, carry):
        tok = pl.ds(pg * 256, 256)
        src = xin[pg].reshape(256, 2 * D)
        qkv = jnp.dot(src[:, :D], w_v[:, 0:896], preferred_element_type=F32)
        od = jnp.dot(src[:, D:], w_v[:, 768:1152], preferred_element_type=F32)
        qa = qkv[:, 0:384].astype(BF)
        ka = turn(qkv[:, 256:640], -32).astype(BF)
        va = turn(qkv[:, 512:896], -64).astype(BF)
        da = turn(od, -96).astype(BF)
        dq, dk, dv, att = attention(qa, ka, va, da)
        dk, dv, att = turn(dk, 32), turn(dv, 64), turn(att, 96)
        tiles = [[] for _ in range(9)]
        for start, val in ((0, dq), (2, dk), (4, dv), (6, att)):
            for t in range(3):
                tiles[start + t].append(val[:, 128 * t : 128 * (t + 1)])
        for t in range(9):
            g_v[tok, 128 * t : 128 * (t + 1)] = functools.reduce(lambda a, b: a + b, tiles[t]).astype(BF)
        left = jnp.where(lane < 864, g_v[tok, 0:896], jnp.zeros((256, 896), BF))
        dn[pg] = nt(left, w_v[:, 0:896]).astype(BF)
        swap_dn(pg).start()
        return carry

    lax.fori_loop(0, 2, tokens, 0)

    def grads(i):
        a = tn(xin[:, :, :, :, pl.ds(pl.multiple_of(128 * i, 128), 128)].reshape(512, 128), g_v[:, 0:896])
        b = tn(
            xin[:, :, :, :, pl.ds(pl.multiple_of(D + 128 * i, 128), 128)].reshape(512, 128),
            g_v[:, 768:1152],
        )
        lane = lax.broadcasted_iota(jnp.int32, (1, 128), 1)
        mid = jnp.where(lane < 96, a[:, 768:896], b[:, 0:128])
        return jnp.concatenate([a[:, 0:768], mid, b[:, 128:384]], 1)

    def grad_rows(i, carry):
        block = grads(i).astype(BF).reshape(2, 4, 16, D)
        xx = i // 4
        for e in range(2):
            zz = 2 * (i % 4) + e
            o = (zz + 8 - z) % 8
            slot = (o // 4) * (15 - 4 * o) + 2 * o
            dw_p[xx, slot, :, :, 0:SP] = block[e, :, :, :SP]
            dw_q[zz, xx] = block[e, :, :, SP:]
        return carry

    lax.fori_loop(0, 8, grad_rows, 0)

    def q_own(o):
        return dw_q.at[(z + o) % 8]

    q_ring = {(0, 0): [net.start(dw_q.at[(z + 4) % 8, 0], rq.at[0, 0, 0], z_up)]}
    q_ring[1, 1] = [net.start(dw_q.at[(z + 4) % 8, 1], rq.at[1, 0, 1], z_dn)]
    for i, o, peer in ((0, 3, z_up), (1, 5, z_dn)):
        q_ring[i, 1 - i] = [net.start(dw_q.at[(z + o) % 8, 1 - i], rq.at[i, 1, 1 - i], peer)]

    def q_step(s):
        for i, o, peer in ((0, 4 - s, z_up), (1, 4 + s, z_dn)):
            for half in (i, 1 - i):
                if s == 1 and half != i:
                    continue
                q_ring[i, half][-1].wait_recv()
                t = q_own(o)[half].astype(F32) + rq[i, s - 1, half].astype(F32)
                tq[i, s - 1, half] = t.astype(BF)
                q_ring[i, half].append(net.start(tq.at[i, s - 1, half], rq.at[i, s, half], peer))

    for pg in range(2):
        swap_dn(pg).wait_recv()
    ps[...] = (dn[:, here].astype(F32) + rs[...].astype(F32)).astype(BF)
    dn_h = net.start(ps.at[1 - h], rh, h_peer)

    rest = grads(8)
    for r in range(2):
        f_v[...] = jnp.zeros((1024, 128), F32)
        for j in range(9):
            f_v[pl.ds(j, 64, stride=16), :] = rest[64 * r : 64 * r + 64, 128 * j : 128 * (j + 1)]
        for xx in range(2):
            for j in range(8):
                k = pl.ds(pl.multiple_of((xx * 8 + (z + OFFS[j]) % 8) * 64, 64), 64)
                dw_p[xx, j, :, :, SP + 128 * r : SP + 128 * (r + 1)] = (
                    f_v[k, :].astype(BF).reshape(4, 16, 128)
                )

    sums = {}
    for g in (3, 2, 1, 0):
        for i, xx in enumerate((1 - x, x)):
            at = GROUPS[g]
            sums[g, i] = RowSum(
                net, (lambda d, xx=xx, at=at: dw_p.at[xx, at, (y + d) % 4]),
                far_p.at[i, at], (got_p.at[i, 0, at], got_p.at[i, 1, at]), both_p.at[i, at],
                y_up, y_dn, i == 0,
            )

    def y_first(g):
        for i in range(2):
            sums[g, i].first()

    def y_second(g):
        for i in range(2):
            sums[g, i].second()

    x_c, z_s = {}, {}

    def y_total(g):
        at = GROUPS[g]
        pyp[0, at] = sums[g, 0].total().astype(BF)
        x_c[g] = net.start(pyp.at[0, at], rxp.at[at], x_peer)
        pyp[1, at] = sums[g, 1].total().astype(BF)

    def x_total(g):
        at = GROUPS[g]
        x_c[g].wait_recv()
        pxp[at] = (pyp[1, at].astype(F32) + rxp[at].astype(F32)).astype(BF)
        for j in range(at.start, at.start + at.size):
            if j:
                z_s[j] = net.start(pxp.at[j], rzp.at[j - 1], z_peers[OFFS[j] - 1])

    y_first(3)
    y_first(2)
    q_step(1)
    y_second(3)
    y_first(1)
    q_step(2)
    dn_h.wait_recv()
    mine = ps[h].astype(F32) + rh[...].astype(F32)
    mine = mine.astype(BF).astype(F32)
    ghat = xin[h, pl.ds(4 * core, 4), :, :, 0:D].reshape(128, D).astype(F32)
    one = jnp.mean(mine, -1, keepdims=True)
    two = jnp.mean(mine * ghat, -1, keepdims=True)
    res_v[...] = (mine - one - ghat * two).astype(BF).reshape(8, 16, D)

    local = zl == core

    def owner(i):
        to = (member + i) % 8
        target = (base + 8 * core + to, h)
        return remote(res_v.at[to], og.at[ck, h], o_send.at[i], o_recv.at[ck], target)

    stay = pltpu.make_async_copy(res_v.at[member % 8], og.at[ck, h], l_sem.at[1])
    pl.when(jnp.logical_not(local))(lambda: owner(0).start())
    pl.when(local)(lambda: stay.start())
    for i in range(1, 8):
        owner(i).start()

    y_second(2)
    y_total(3)
    y_first(0)
    y_second(1)
    q_step(3)
    y_total(2)
    x_total(3)
    y_second(0)

    def out_share(part):
        for c in range(4 * part, 4 * part + 4):
            got = remote(res_v.at[0], og.at[c, h], o_send.at[0], o_recv.at[c], h_peer)
            pl.when(jnp.logical_not(local & (ck == c)))(lambda got=got: got.wait_recv())
            pl.when(local & (ck == c))(lambda: stay.wait())
        at = og.at[pl.ds(4 * part, 4), h]
        return net.start(at, at, h_peer)

    y_total(1)
    o_h = [out_share(0)]
    x_total(2)
    y_total(0)
    o_h.append(out_share(1))
    for c in q_ring.values():
        c[-1].wait_recv()
    t = q_own(0)[...].astype(F32) + rq[0, 3].astype(F32) + rq[1, 3].astype(F32)
    zq[...] = t.astype(BF)
    q_sums = []
    for i in range(2):
        at = pl.ds(i, 1)
        q_sums.append(
            RowSum(
                net, (lambda d, at=at: zq.at[at, (y + d) % 4]),
                far_q.at[at], (got_q.at[0, at], got_q.at[1, at]), both_q.at[at],
                y_up, y_dn, i == 0,
            )
        )
        q_sums[i].first()
    x_total(1)
    for i in range(2):
        q_sums[i].second()
    x_total(0)
    for i in range(2):
        pq[i] = q_sums[i].total()[0].astype(BF)
    q_x2 = net.start(pq.at[1 - x], rxq, x_peer)

    for c in o_h:
        c.wait_recv()
    back = nt(og[...].reshape(256, D), perm_v[...])
    for f in range(2):
        nat = jnp.concatenate([back[16 * g + 8 * f : 16 * g + 8 * f + 8] for g in range(16)], 0)
        nat = up_ref[f].astype(F32) + rstd_v[128 * f : 128 * f + 128] * nat
        out[f] = nat.astype(BF)

    t = pxp[0].astype(F32)
    for j in range(1, 8):
        z_s[j].wait_recv()
        t = t + rzp[j - 1].astype(F32)
    fin_v[:, 0:SP] = t[:, :SP]
    fin_v[:, D:BLK] = t[:, SP:]
    q_x2.wait_recv()
    fin_v[:, SP:D] = pq[x].astype(F32) + rxq[...].astype(F32)
    last = net.start(fin_v, fsib_v, sibling)
    last.wait()

    mine, other = fin_v[...], fsib_v[...]
    rows = []
    for half in (jnp.where(core == 0, mine, other), jnp.where(core == 0, other, mine)):
        main = jnp.where(core == 0, half[0:8, :D], half[8:16, :D])
        tail = jnp.where(core == 0, half[0:9, D : D + 128], half[0:9, D + 128 :])
        tail = jnp.concatenate([tail[j : j + 1] for j in range(9)], 1)
        rows.append(jnp.concatenate([main, tail], 0))
    for t in range(4):
        both = jnp.concatenate([r[:, 288 * t : 288 * t + 288] for r in rows], 1)
        if t < 3:
            gq[:, t, :] = both
        else:
            go[...] = both

    pl.when(jnp.logical_not(local))(lambda: owner(0).wait_send())
    for i in range(1, 8):
        owner(i).wait_send()
    for pg in range(2):
        swap_dn(pg).wait_send()
    for t in sent:
        for c in t.values():
            c.wait_send()
    rest = o_h + [q_x, q_f0, q_f1, dn_h, q_x2] + q_c + t_h + t_s
    for c in ring_up + ring_dn + list(q_ring.values()):
        rest = rest + c
    for c in rest + list(tok.values()) + list(tok_z.values()) + list(z_c.values()) + list(x_c.values()) + list(z_s.values()):
        c.wait_send()
    for c in q_sums + list(sums.values()):
        c.end()


def on_device(inputs, out_grad, gate, qkv_weight, out_weight):
    vm = pl.BlockSpec(memory_space=pltpu.VMEM)
    hbm = pl.BlockSpec(memory_space=pl.ANY)
    dma = pltpu.SemaphoreType.DMA
    shape = jax.ShapeDtypeStruct
    bf = lambda *dims: pltpu.VMEM(dims, BF)
    f32 = lambda *dims: pltpu.VMEM(dims, F32)
    grad_inputs, grad_qkv, grad_out = pl.pallas_call(
        kernel,
        out_shape=[shape((2, 128, D), BF), shape((9, 3, 576), F32), shape((9, 576), F32)],
        in_specs=[hbm] * 2 + [vm] * 3,
        out_specs=[vm] * 3,
        scratch_shapes=[
            bf(2, 128, D), bf(2, 128, D),
            bf(16, BLK), bf(16, BLK), bf(16, GW), bf(16, GQ), bf(2, 256, D), bf(16, 16, 2 * D), bf(D, D),
            f32(256, 1), bf(XS, ZS, YS, 16, GW), bf(ZS, XS, YS, 16, GQ), bf(2, 8, 2, 16, 2 * D),
            bf(D, D), bf(512, D), f32(1024, 128), bf(XS, ZS, YS, 16, SW), bf(ZS, XS, YS, 16, SQ),
            bf(2, 256, D), bf(2, 128, D), bf(2, 128, D), bf(128, D), bf(8, 16, D), bf(8, 2, 16, D),
            bf(2, ZS, 16, SW), bf(2, 2, ZS, 16, SW), bf(2, ZS, 16, SW), bf(2, ZS, 16, SW),
            bf(ZS, 16, SW), bf(ZS, 16, SW), bf(7, 16, SW),
            bf(2, 4, XS, YS, 16, SQ), bf(2, 3, XS, YS, 16, SQ), bf(XS, YS, 16, SQ),
            bf(2, 16, SQ), bf(2, 2, 16, SQ), bf(2, 16, SQ), bf(2, 16, SQ), bf(16, SQ),
            f32(16, BLK), f32(16, BLK),
            dma((150,)), dma((150,)), dma((8,)), dma((8,)), dma((2,)), dma((2,)), dma((4,)),
        ],
        compiler_params=pltpu.CompilerParams(
            collective_id=0, has_side_effects=True, vmem_limit_bytes=VMEM_BYTES
        ),
        name="sublayer_backward",
    )(inputs, out_grad, gate, qkv_weight, out_weight)
    return grad_inputs, grad_qkv, grad_out


def solution(mesh):
    in_specs = (
        P("seq", None, None),
        P("seq", None, None),
        P(),
        P("seq", None, "head"),
        P("seq", "head"),
    )
    out_specs = (P("seq", None, None), P("seq", None, "head"), P("seq", "head"))
    return jax.shard_map(
        on_device, mesh=mesh, in_specs=in_specs, out_specs=out_specs, check_vma=False
    )
```

```python
import functools

import jax
import jax.numpy as jnp
from jax import lax
from jax.experimental import pallas as pl
from jax.experimental.pallas import tpu as pltpu
from jax.sharding import PartitionSpec as P

D = 1152
HEAD_DIM = 72
LOG2E = 1.4426950408889634
XS, ZS, YS = 2, 8, 4
CHIPS = XS * ZS * YS
BLK = 1408
GP, SP = 512, 640
GW, SW = GP + BLK - D, SP + BLK - D
GQ, SQ = D - GP, D - SP
OFFS = (0, 7, 1, 6, 2, 5, 3, 4)
SLOT = tuple(OFFS.index(d) for d in range(8))
GROUPS = (pl.ds(0, 1), pl.ds(1, 2), pl.ds(3, 2), pl.ds(5, 3))
MESH = pl.DeviceIdType.MESH
BF = jnp.bfloat16
F32 = jnp.float32
VMEM_BYTES = 58 * 2**20


def place():
    s = lax.axis_index("seq")
    h = lax.axis_index("head")
    return s // 64, (s // 8) % 8, (s // 2) % 4, s % 2, h


def seq_of(x, z, y, core):
    return ((x * 8 + z) * 4 + y) * 2 + core


def signal(sem, target):
    pl.semaphore_signal(sem, inc=1, device_id=target, device_id_type=MESH)


def remote(src, dst, send, recv, target):
    return pltpu.make_async_remote_copy(
        src_ref=src, dst_ref=dst, send_sem=send, recv_sem=recv, device_id=target, device_id_type=MESH
    )


def permuted_feature(shape, dim):
    f = lax.broadcasted_iota(jnp.int32, shape, dim)
    owner = f // 9
    q = f - owner * 9
    return jnp.where(q < 8, owner * 8 + q, 1024 + (owner % 2) * 64 + owner // 2)


class Copies:
    def __init__(self, send, recv):
        self.send, self.recv, self.count = send, recv, 0

    def start(self, src, dst, target):
        k = self.count
        self.count += 1
        c = remote(src, dst, self.send.at[k], self.recv.at[k], target)
        c.start()
        return c


class RowSum:
    def __init__(self, net, src, far, got, both, up, down, by_up):
        self.net, self.src, self.far, self.got, self.both = net, src, far, got, both
        self.up, self.down, self.by_up = up, down, by_up

    def first(self):
        net, src = self.net, self.src
        if self.by_up:
            self.c = [net.start(src(2), self.far, self.up), net.start(src(3), self.got[1], self.down)]
        else:
            self.c = [net.start(src(2), self.far, self.down), net.start(src(1), self.got[0], self.up)]

    def second(self):
        self.c[0].wait_recv()
        t = self.src(1 if self.by_up else 3)[...].astype(F32) + self.far[...].astype(F32)
        self.both[...] = t.astype(BF)
        if self.by_up:
            self.c.append(self.net.start(self.both, self.got[0], self.up))
        else:
            self.c.append(self.net.start(self.both, self.got[1], self.down))

    def total(self):
        self.c[1].wait_recv()
        self.c[2].wait_recv()
        t = self.src(0)[...].astype(F32)
        return t + self.got[0][...].astype(F32) + self.got[1][...].astype(F32)

    def end(self):
        for c in self.c:
            c.wait_send()


def normalise(v):
    mean = jnp.mean(v, -1, keepdims=True)
    centered = v - mean
    rstd = lax.rsqrt(jnp.mean(centered * centered, -1, keepdims=True) + 1e-06)
    return centered * rstd, rstd


def turn(v, by):
    return jnp.concatenate([v[:, -by:], v[:, :-by]], 1)


def nt(a, b):
    return lax.dot_general(a, b, (((1,), (1,)), ((), ())), preferred_element_type=F32)


def tn(a, b):
    return lax.dot_general(a, b, (((0,), (0,)), ((), ())), preferred_element_type=F32)


def attention(qa, ka, va, da):
    scale = HEAD_DIM ** (-0.5)
    rows = lax.broadcasted_iota(jnp.int32, (256, 256), 0)
    cols = lax.broadcasted_iota(jnp.int32, (256, 256), 1)
    same = (rows & 7) == (cols & 7)
    outs = [[[] for _ in range(3)] for _ in range(4)]
    for head, (lo, hi) in enumerate(((0, 128), (0, 256), (128, 256), (128, 384))):
        lane = lax.broadcasted_iota(jnp.int32, (1, hi - lo), 1) + lo
        keep = (lane >= HEAD_DIM * head) & (lane < HEAD_DIM * (head + 1))
        q, k, v, d = (a[:, lo:hi] for a in (qa, ka, va, da))
        km = jnp.where(keep, k, jnp.zeros_like(k))
        vm = jnp.where(keep, v, jnp.zeros_like(v))
        scores = jnp.where(same, nt(km, q), -1e30)
        top = jnp.max(scores, 0, keepdims=True)
        e = jnp.exp2((scores - top) * (scale * LOG2E))
        probs = e * (1.0 / jnp.sum(e, 0, keepdims=True))
        probs_b = probs.astype(BF)
        att = tn(probs_b, v).astype(BF)
        dprobs = nt(vm, d)
        delta = jnp.sum(probs_b.astype(F32) * dprobs, 0, keepdims=True)
        ds = (probs * (dprobs - delta) * scale).astype(BF)
        dq = tn(ds, k)
        dk = jnp.dot(ds, q, preferred_element_type=F32)
        dv = jnp.dot(probs_b, d, preferred_element_type=F32)
        for slot, val in zip(outs, (dq, dk, dv, att.astype(F32))):
            val = jnp.where(keep, val, 0.0)
            for t in range(lo // 128, hi // 128):
                slot[t].append(val[:, t * 128 - lo : t * 128 - lo + 128])
    return [jnp.concatenate([functools.reduce(lambda a, b: a + b, t) for t in s], 1) for s in outs]


def kernel(
    in_hbm, up_hbm, gate_ref, wq_ref, wo_ref, out, gq, go,
    in_ref, up_ref, sib_v, away_v, mine_p, mine_q, nat_v, xg_v, perm_v, rstd_v, buf_p, buf_q, xin,
    w_v, g_v, f_v, dw_p, dw_q, dn, rs, ps, rh, res_v, og,
    far_p, got_p, both_p, pyp, rxp, pxp, rzp, rq, tq, zq, far_q, got_q, both_q, pq, rxq, fin_v, fsib_v,
    send_sem, recv_sem, o_send, o_recv, s_send, s_recv, l_sem,
):
    x, z, y, core, h = place()
    zl = z % 2
    ck = zl * 4 + y
    member = ck * 2 + core
    base = (x * 8 + (z // 2) * 2) * 8
    above, below, far = (y + 1) % 4, (y + 3) % 4, (y + 2) % 4
    sibling = (seq_of(x, z, y, 1 - core), h)
    x_peer = (seq_of(1 - x, z, y, core), h)
    h_peer = (seq_of(x, z, y, core), 1 - h)
    y_up = (seq_of(x, z, above, core), h)
    y_dn = (seq_of(x, z, below, core), h)
    z_up = (seq_of(x, (z + 1) % 8, y, core), h)
    z_dn = (seq_of(x, (z + 7) % 8, y, core), h)
    z_peers = [(seq_of(x, (z + d) % 8, y, core), h) for d in range(1, 8)]
    plane, other = pl.ds(zl * 4, 4), pl.ds((1 - zl) * 4, 4)
    zb = (z // 2) * 2
    near_peers = [(seq_of(x, z, yy, core), h) for yy in [(y + d) % 4 for d in range(1, 4)]]
    cross_peers = [(seq_of(x, zb + 1 - zl, yy, core), h) for yy in [(y + d) % 4 for d in range(4)]]
    group = [(base + (member + i) % 16, h) for i in range(1, 16)]
    everyone = [x_peer, h_peer] + z_peers + group
    net = Copies(send_sem, recv_sem)
    barrier = pltpu.get_barrier_semaphore()
    for peer in everyone:
        signal(barrier, peer)

    load = [
        pltpu.make_async_copy(in_hbm, in_ref, l_sem.at[2]),
        pltpu.make_async_copy(up_hbm, up_ref, l_sem.at[3]),
    ]
    for c in load:
        c.start()

    wq, wo = wq_ref[...].astype(F32), wo_ref[...].astype(F32)
    blocks = []
    for half in range(2):
        c = slice(288 * half, 288 * half + 288)
        rows = jnp.concatenate([wq[:, 0, c], wq[:, 1, c], wq[:, 2, c], wo[:, c]], 1)
        main, last = rows[0:8], rows[8:9]
        last = [last[:, 128 * j : 128 * j + 128] for j in range(9)] + [jnp.zeros((7, 128), F32)]
        last = jnp.concatenate(last, 0)
        main0 = jnp.concatenate([main, jnp.zeros((8, D), F32)], 0)
        main1 = jnp.concatenate([jnp.zeros((8, D), F32), main], 0)
        none = jnp.zeros((16, 128), F32)
        block0 = jnp.concatenate([main0, last, none], 1)
        block1 = jnp.concatenate([main1, none, last], 1)
        blocks.append(jnp.where(core == 0, block0, block1))
    away_v[...] = jnp.where(core == 0, blocks[1], blocks[0]).astype(BF)
    mine = jnp.where(core == 0, blocks[0], blocks[1])
    row = permuted_feature((D, 1), 0)
    col = lax.broadcasted_iota(jnp.int32, (1, D), 1)
    perm_v[...] = jnp.where(row == col, 1.0, 0.0).astype(BF)
    for c in load:
        c.wait()
    ghat, rstd = normalise(in_ref[...].reshape(256, D).astype(F32))
    rstd_v[...] = rstd
    nat_v[0] = ghat.astype(BF)
    nat_v[1] = (gate_ref[...].reshape(1, D) * up_ref[...].reshape(256, D).astype(F32)).astype(BF)
    pl.semaphore_wait(barrier, len(everyone))

    swap = net.start(away_v, sib_v, sibling)
    for i in range(2):
        p = jnp.dot(nat_v[i], perm_v[...], preferred_element_type=F32)
        for g in range(16):
            part = jnp.concatenate([p[8 * g : 8 * g + 8], p[128 + 8 * g : 136 + 8 * g]], 0)
            xg_v[g, :, i * D : (i + 1) * D] = part.astype(BF)
    swap.wait()
    mine = (mine + sib_v[...].astype(F32)).astype(BF)
    own_q = mine[:, GP:D]
    mine_p[:, 0:GP] = mine[:, :GP]
    mine_p[:, GP:GW] = mine[:, D:]
    mine_q[...] = own_q
    buf_p[x, 0, y, :, 0:GP] = mine[:, :GP]
    buf_p[x, 0, y, :, GP:GW] = mine[:, D:]
    buf_q[z, x, y] = own_q
    q_x = net.start(mine_q, buf_q.at[z, x, y], x_peer)
    sent = [{} for _ in GROUPS]

    def first(g):
        own = buf_p.at[x, GROUPS[g], y]
        for way, peer in (("up", y_up), ("dn", y_dn), ("x", x_peer)):
            sent[g][way] = net.start(own, own, peer)

    z_c = {}

    def z_send(d):
        z_c[d] = net.start(mine_p, buf_p.at[x, SLOT[8 - d], y], z_peers[d - 1])

    def arrived(g):
        for j in range(GROUPS[g].start, GROUPS[g].start + GROUPS[g].size):
            z_c[8 - OFFS[j]].wait_recv()

    def second(g):
        t = sent[g]
        t["up"].wait_recv()
        got = buf_p.at[x, GROUPS[g], below]
        t["f"] = net.start(got, got, y_up)
        t["x"].wait_recv()
        own = buf_p.at[1 - x, GROUPS[g], y]
        t["oup"] = net.start(own, own, y_up)
        t["odn"] = net.start(own, own, y_dn)

    def third(g):
        t = sent[g]
        t["odn"].wait_recv()
        got = buf_p.at[1 - x, GROUPS[g], above]
        t["of"] = net.start(got, got, y_dn)

    def pass_on(at, peer):
        return net.start(at, at, peer)

    tok, tok_z = {}, {}

    def tok_near(d):
        to = zl * 4 + (y + d) % 4
        tok[d] = net.start(xg_v.at[pl.ds(2 * to, 2)], xin.at[:, ck, core], near_peers[d - 1])

    def tok_cross(d):
        to = (1 - zl) * 4 + (y + d) % 4
        tok_z[d] = net.start(xg_v.at[2 * to + h], xin.at[h, ck, core], cross_peers[d])

    t_h = []

    def tok_share(d):
        tok_z[d].wait_recv()
        t_h.append(pass_on(xin.at[h, (1 - zl) * 4 + (y + 4 - d) % 4, core], h_peer))

    for d in (1, 7, 2, 6, 3, 5, 4):
        z_send(d)
    first(0)
    own_t = pltpu.make_async_copy(xg_v.at[pl.ds(2 * ck, 2)], xin.at[:, ck, core], l_sem.at[0])
    own_t.start()
    q_x.wait_recv()
    q_c = [pass_on(buf_q.at[z, :, y], y_up), pass_on(buf_q.at[z, :, y], y_dn)]
    arrived(1)
    first(1)
    q_c[0].wait_recv()
    q_f0 = pass_on(buf_q.at[z, 0, below], y_up)
    q_c[1].wait_recv()
    q_f1 = pass_on(buf_q.at[z, 1, above], y_dn)
    tok_cross(0)
    tok_cross(2)
    arrived(2)
    first(2)
    second(0)
    q_f0.wait_recv()
    q_f1.wait_recv()
    ring_up, ring_dn = [[], []], [[], []]
    for i in range(2):
        ring_up[i].append(pass_on(buf_q.at[z, i], z_up))
        ring_dn[i].append(pass_on(buf_q.at[z, i], z_dn))

    def ring(step):
        for i in range(2):
            ring_up[i][-1].wait_recv()
            if step < 3 or i == 0:
                ring_up[i].append(pass_on(buf_q.at[(z + 8 - step) % 8, i], z_up))
            ring_dn[i][-1].wait_recv()
            if step < 3 or i == 1:
                ring_dn[i].append(pass_on(buf_q.at[(z + step) % 8, i], z_dn))

    tok_cross(1)
    tok_cross(3)
    arrived(3)
    first(3)
    second(1)
    tok_near(1)
    tok_near(3)
    tok_share(0)
    tok_share(2)
    ring(1)
    third(0)
    second(2)
    tok_near(2)
    tok_share(1)
    tok_share(3)
    third(1)
    ring(2)
    second(3)
    own_t.wait()
    for d in (1, 3, 2):
        tok[d].wait_recv()
    t_s = [pass_on(xin.at[:, plane, core], sibling)]
    third(2)
    for c in t_h:
        c.wait_recv()
    t_s.append(pass_on(xin.at[:, other, core], sibling))
    ring(3)
    third(3)
    ring_up[0][-1].wait_recv()
    ring_dn[1][-1].wait_recv()
    for g, t in enumerate(sent):
        for name in ("dn", "f", "of", "oup"):
            t[name].wait_recv()
    for c in t_s:
        c.wait_recv()

    for xx in range(2):
        for j in range(8):
            k = pl.ds(pl.multiple_of((xx * 8 + (z + OFFS[j]) % 8) * 64, 64), 64)
            w_v[k, 0:GP] = buf_p[xx, j, :, :, 0:GP].reshape(64, GP)
        for zz in range(8):
            k = (xx * 8 + zz) * 64
            w_v[k : k + 64, GP:D] = buf_q[zz, xx].reshape(64, GQ)
    for r in range(2):
        for xx in range(2):
            for j in range(8):
                k = pl.ds(pl.multiple_of((xx * 8 + (z + OFFS[j]) % 8) * 64, 64), 64)
                part = buf_p[xx, j, :, :, GP + 128 * r : GP + 128 * (r + 1)]
                f_v[k, :] = part.reshape(64, 128).astype(F32)
        for j in range(9):
            w_v[1024 + 64 * r : 1088 + 64 * r, 128 * j : 128 * (j + 1)] = f_v[
                pl.ds(j, 64, stride=16), :
            ].astype(BF)

    lane = lax.broadcasted_iota(jnp.int32, (1, 896), 1)
    away = pl.ds(pl.multiple_of((1 - core) * 128, 128), 128)
    here = pl.ds(pl.multiple_of(core * 128, 128), 128)

    def swap_dn(pg):
        return remote(dn.at[pg, away], rs.at[pg], s_send.at[pg], s_recv.at[pg], sibling)

    def tokens(pg):
        tok = slice(pg * 256, pg * 256 + 256)
        src = xin[pg].reshape(256, 2 * D)
        qkv = jnp.dot(src[:, :D], w_v[:, 0:896], preferred_element_type=F32)
        od = jnp.dot(src[:, D:], w_v[:, 768:1152], preferred_element_type=F32)
        qa = qkv[:, 0:384].astype(BF)
        ka = turn(qkv[:, 256:640], -32).astype(BF)
        va = turn(qkv[:, 512:896], -64).astype(BF)
        da = turn(od, -96).astype(BF)
        dq, dk, dv, att = attention(qa, ka, va, da)
        dk, dv, att = turn(dk, 32), turn(dv, 64), turn(att, 96)
        tiles = [[] for _ in range(9)]
        for start, val in ((0, dq), (2, dk), (4, dv), (6, att)):
            for t in range(3):
                tiles[start + t].append(val[:, 128 * t : 128 * (t + 1)])
        for t in range(9):
            g_v[tok, 128 * t : 128 * (t + 1)] = functools.reduce(lambda a, b: a + b, tiles[t]).astype(BF)

    tokens(0)
    tokens(1)

    def grads(i):
        a = tn(xin[:, :, :, :, pl.ds(pl.multiple_of(128 * i, 128), 128)].reshape(512, 128), g_v[:, 0:896])
        b = tn(
            xin[:, :, :, :, pl.ds(pl.multiple_of(D + 128 * i, 128), 128)].reshape(512, 128),
            g_v[:, 768:1152],
        )
        lane = lax.broadcasted_iota(jnp.int32, (1, 128), 1)
        mid = jnp.where(lane < 96, a[:, 768:896], b[:, 0:128])
        return jnp.concatenate([a[:, 0:768], mid, b[:, 128:384]], 1)

    def grad_rows(i, carry):
        block = grads(i).astype(BF).reshape(2, 4, 16, D)
        xx = i // 4
        for e in range(2):
            zz = 2 * (i % 4) + e
            o = (zz + 8 - z) % 8
            slot = (o // 4) * (15 - 4 * o) + 2 * o
            dw_p[xx, slot, :, :, 0:SP] = block[e, :, :, :SP]
            dw_q[zz, xx] = block[e, :, :, SP:]
        return carry

    lax.fori_loop(0, 8, grad_rows, 0)

    def q_own(o):
        return dw_q.at[(z + o) % 8]

    q_ring = {(0, 0): [net.start(dw_q.at[(z + 4) % 8, 0], rq.at[0, 0, 0], z_up)]}
    q_ring[1, 1] = [net.start(dw_q.at[(z + 4) % 8, 1], rq.at[1, 0, 1], z_dn)]
    for i, o, peer in ((0, 3, z_up), (1, 5, z_dn)):
        q_ring[i, 1 - i] = [net.start(dw_q.at[(z + o) % 8, 1 - i], rq.at[i, 1, 1 - i], peer)]

    def q_step(s):
        for i, o, peer in ((0, 4 - s, z_up), (1, 4 + s, z_dn)):
            for half in (i, 1 - i):
                if s == 1 and half != i:
                    continue
                q_ring[i, half][-1].wait_recv()
                t = q_own(o)[half].astype(F32) + rq[i, s - 1, half].astype(F32)
                tq[i, s - 1, half] = t.astype(BF)
                q_ring[i, half].append(net.start(tq.at[i, s - 1, half], rq.at[i, s, half], peer))

    rest = grads(8)
    for r in range(2):
        f_v[...] = jnp.zeros((1024, 128), F32)
        for j in range(9):
            f_v[pl.ds(j, 64, stride=16), :] = rest[64 * r : 64 * r + 64, 128 * j : 128 * (j + 1)]
        for xx in range(2):
            for j in range(8):
                k = pl.ds(pl.multiple_of((xx * 8 + (z + OFFS[j]) % 8) * 64, 64), 64)
                dw_p[xx, j, :, :, SP + 128 * r : SP + 128 * (r + 1)] = (
                    f_v[k, :].astype(BF).reshape(4, 16, 128)
                )

    sums = {}
    for g in (3, 2, 1, 0):
        for i, xx in enumerate((1 - x, x)):
            at = GROUPS[g]
            sums[g, i] = RowSum(
                net, (lambda d, xx=xx, at=at: dw_p.at[xx, at, (y + d) % 4]),
                far_p.at[i, at], (got_p.at[i, 0, at], got_p.at[i, 1, at]), both_p.at[i, at],
                y_up, y_dn, i == 0,
            )

    def y_first(g):
        for i in range(2):
            sums[g, i].first()

    def y_second(g):
        for i in range(2):
            sums[g, i].second()

    x_c, z_s = {}, {}

    def y_total(g):
        at = GROUPS[g]
        pyp[0, at] = sums[g, 0].total().astype(BF)
        x_c[g] = net.start(pyp.at[0, at], rxp.at[at], x_peer)
        pyp[1, at] = sums[g, 1].total().astype(BF)

    def x_total(g):
        at = GROUPS[g]
        x_c[g].wait_recv()
        pxp[at] = (pyp[1, at].astype(F32) + rxp[at].astype(F32)).astype(BF)
        for j in range(at.start, at.start + at.size):
            if j:
                z_s[j] = net.start(pxp.at[j], rzp.at[j - 1], z_peers[OFFS[j] - 1])

    def partial_dn(pg):
        left = jnp.where(lane < 864, g_v[pg * 256 : pg * 256 + 256, 0:896], jnp.zeros((256, 896), BF))
        dn[pg] = nt(left, w_v[:, 0:896]).astype(BF)
        swap_dn(pg).start()

    y_first(3)
    y_first(2)
    partial_dn(0)
    partial_dn(1)
    q_step(1)
    y_second(3)
    y_first(1)
    for pg in range(2):
        swap_dn(pg).wait_recv()
    ps[...] = (dn[:, here].astype(F32) + rs[...].astype(F32)).astype(BF)
    dn_h = net.start(ps.at[1 - h], rh, h_peer)
    q_step(2)
    y_second(2)
    y_total(3)
    y_first(0)
    y_second(1)
    dn_h.wait_recv()
    mine = ps[h].astype(F32) + rh[...].astype(F32)
    mine = mine.astype(BF).astype(F32)
    ghat = xin[h, pl.ds(4 * core, 4), :, :, 0:D].reshape(128, D).astype(F32)
    one = jnp.mean(mine, -1, keepdims=True)
    two = jnp.mean(mine * ghat, -1, keepdims=True)
    res_v[...] = (mine - one - ghat * two).astype(BF).reshape(8, 16, D)

    local = zl == core

    def owner(i):
        to = (member + i) % 8
        target = (base + 8 * core + to, h)
        return remote(res_v.at[to], og.at[ck, h], o_send.at[i], o_recv.at[ck], target)

    stay = pltpu.make_async_copy(res_v.at[member % 8], og.at[ck, h], l_sem.at[1])
    pl.when(jnp.logical_not(local))(lambda: owner(0).start())
    pl.when(local)(lambda: stay.start())
    for i in range(1, 8):
        owner(i).start()

    q_step(3)
    y_total(2)
    x_total(3)
    y_second(0)

    def out_share(part):
        for c in range(4 * part, 4 * part + 4):
            got = remote(res_v.at[0], og.at[c, h], o_send.at[0], o_recv.at[c], h_peer)
            pl.when(jnp.logical_not(local & (ck == c)))(lambda got=got: got.wait_recv())
            pl.when(local & (ck == c))(lambda: stay.wait())
        at = og.at[pl.ds(4 * part, 4), h]
        return net.start(at, at, h_peer)

    y_total(1)
    o_h = [out_share(0)]
    x_total(2)
    y_total(0)
    o_h.append(out_share(1))
    for c in q_ring.values():
        c[-1].wait_recv()
    t = q_own(0)[...].astype(F32) + rq[0, 3].astype(F32) + rq[1, 3].astype(F32)
    zq[...] = t.astype(BF)
    q_sums = []
    for i in range(2):
        at = pl.ds(i, 1)
        q_sums.append(
            RowSum(
                net, (lambda d, at=at: zq.at[at, (y + d) % 4]),
                far_q.at[at], (got_q.at[0, at], got_q.at[1, at]), both_q.at[at],
                y_up, y_dn, i == 0,
            )
        )
        q_sums[i].first()
    x_total(1)
    for i in range(2):
        q_sums[i].second()
    x_total(0)
    for i in range(2):
        pq[i] = q_sums[i].total()[0].astype(BF)
    q_x2 = net.start(pq.at[1 - x], rxq, x_peer)

    for c in o_h:
        c.wait_recv()
    back = nt(og[...].reshape(256, D), perm_v[...])
    for f in range(2):
        nat = jnp.concatenate([back[16 * g + 8 * f : 16 * g + 8 * f + 8] for g in range(16)], 0)
        nat = up_ref[f].astype(F32) + rstd_v[128 * f : 128 * f + 128] * nat
        out[f] = nat.astype(BF)

    t = pxp[0].astype(F32)
    for j in range(1, 8):
        z_s[j].wait_recv()
        t = t + rzp[j - 1].astype(F32)
    fin_v[:, 0:SP] = t[:, :SP]
    fin_v[:, D:BLK] = t[:, SP:]
    q_x2.wait_recv()
    fin_v[:, SP:D] = pq[x].astype(F32) + rxq[...].astype(F32)
    last = net.start(fin_v, fsib_v, sibling)
    last.wait()

    mine, other = fin_v[...], fsib_v[...]
    rows = []
    for half in (jnp.where(core == 0, mine, other), jnp.where(core == 0, other, mine)):
        main = jnp.where(core == 0, half[0:8, :D], half[8:16, :D])
        tail = jnp.where(core == 0, half[0:9, D : D + 128], half[0:9, D + 128 :])
        tail = jnp.concatenate([tail[j : j + 1] for j in range(9)], 1)
        rows.append(jnp.concatenate([main, tail], 0))
    for t in range(4):
        both = jnp.concatenate([r[:, 288 * t : 288 * t + 288] for r in rows], 1)
        if t < 3:
            gq[:, t, :] = both
        else:
            go[...] = both

    pl.when(jnp.logical_not(local))(lambda: owner(0).wait_send())
    for i in range(1, 8):
        owner(i).wait_send()
    for pg in range(2):
        swap_dn(pg).wait_send()
    for t in sent:
        for c in t.values():
            c.wait_send()
    rest = o_h + [q_x, q_f0, q_f1, dn_h, q_x2] + q_c + t_h + t_s
    for c in ring_up + ring_dn + list(q_ring.values()):
        rest = rest + c
    for c in rest + list(tok.values()) + list(tok_z.values()) + list(z_c.values()) + list(x_c.values()) + list(z_s.values()):
        c.wait_send()
    for c in q_sums + list(sums.values()):
        c.end()


def on_device(inputs, out_grad, gate, qkv_weight, out_weight):
    vm = pl.BlockSpec(memory_space=pltpu.VMEM)
    hbm = pl.BlockSpec(memory_space=pl.ANY)
    dma = pltpu.SemaphoreType.DMA
    shape = jax.ShapeDtypeStruct
    bf = lambda *dims: pltpu.VMEM(dims, BF)
    f32 = lambda *dims: pltpu.VMEM(dims, F32)
    grad_inputs, grad_qkv, grad_out = pl.pallas_call(
        kernel,
        out_shape=[shape((2, 128, D), BF), shape((9, 3, 576), F32), shape((9, 576), F32)],
        in_specs=[hbm] * 2 + [vm] * 3,
        out_specs=[vm] * 3,
        scratch_shapes=[
            bf(2, 128, D), bf(2, 128, D),
            bf(16, BLK), bf(16, BLK), bf(16, GW), bf(16, GQ), bf(2, 256, D), bf(16, 16, 2 * D), bf(D, D),
            f32(256, 1), bf(XS, ZS, YS, 16, GW), bf(ZS, XS, YS, 16, GQ), bf(2, 8, 2, 16, 2 * D),
            bf(D, D), bf(512, D), f32(1024, 128), bf(XS, ZS, YS, 16, SW), bf(ZS, XS, YS, 16, SQ),
            bf(2, 256, D), bf(2, 128, D), bf(2, 128, D), bf(128, D), bf(8, 16, D), bf(8, 2, 16, D),
            bf(2, ZS, 16, SW), bf(2, 2, ZS, 16, SW), bf(2, ZS, 16, SW), bf(2, ZS, 16, SW),
            bf(ZS, 16, SW), bf(ZS, 16, SW), bf(7, 16, SW),
            bf(2, 4, XS, YS, 16, SQ), bf(2, 3, XS, YS, 16, SQ), bf(XS, YS, 16, SQ),
            bf(2, 16, SQ), bf(2, 2, 16, SQ), bf(2, 16, SQ), bf(2, 16, SQ), bf(16, SQ),
            f32(16, BLK), f32(16, BLK),
            dma((150,)), dma((150,)), dma((8,)), dma((8,)), dma((2,)), dma((2,)), dma((4,)),
        ],
        compiler_params=pltpu.CompilerParams(
            collective_id=0, has_side_effects=True, vmem_limit_bytes=VMEM_BYTES
        ),
        name="sublayer_backward",
    )(inputs, out_grad, gate, qkv_weight, out_weight)
    return grad_inputs, grad_qkv, grad_out


def solution(mesh):
    in_specs = (
        P("seq", None, None),
        P("seq", None, None),
        P(),
        P("seq", None, "head"),
        P("seq", "head"),
    )
    out_specs = (P("seq", None, None), P("seq", None, "head"), P("seq", "head"))
    return jax.shard_map(
        on_device, mesh=mesh, in_specs=in_specs, out_specs=out_specs, check_vma=False
    )
```

```python
import functools

import jax
import jax.numpy as jnp
from jax import lax
from jax.experimental import pallas as pl
from jax.experimental.pallas import tpu as pltpu
from jax.sharding import PartitionSpec as P

D = 1152
HEAD_DIM = 72
LOG2E = 1.4426950408889634
XS, ZS, YS = 2, 8, 4
CHIPS = XS * ZS * YS
BLK = 1408
GP, SP = 512, 640
GW, SW = GP + BLK - D, SP + BLK - D
GQ, SQ = D - GP, D - SP
OFFS = (0, 7, 1, 6, 2, 5, 3, 4)
SLOT = tuple(OFFS.index(d) for d in range(8))
GROUPS = (pl.ds(0, 1), pl.ds(1, 2), pl.ds(3, 2), pl.ds(5, 3))
MESH = pl.DeviceIdType.MESH
BF = jnp.bfloat16
F32 = jnp.float32
VMEM_BYTES = 58 * 2**20


def place():
    s = lax.axis_index("seq")
    h = lax.axis_index("head")
    return s // 64, (s // 8) % 8, (s // 2) % 4, s % 2, h


def seq_of(x, z, y, core):
    return ((x * 8 + z) * 4 + y) * 2 + core


def signal(sem, target):
    pl.semaphore_signal(sem, inc=1, device_id=target, device_id_type=MESH)


def remote(src, dst, send, recv, target):
    return pltpu.make_async_remote_copy(
        src_ref=src, dst_ref=dst, send_sem=send, recv_sem=recv, device_id=target, device_id_type=MESH
    )


def permuted_feature(shape, dim):
    f = lax.broadcasted_iota(jnp.int32, shape, dim)
    owner = f // 9
    q = f - owner * 9
    return jnp.where(q < 8, owner * 8 + q, 1024 + (owner % 2) * 64 + owner // 2)


class Copies:
    def __init__(self, send, recv):
        self.send, self.recv, self.count = send, recv, 0

    def start(self, src, dst, target):
        k = self.count
        self.count += 1
        c = remote(src, dst, self.send.at[k], self.recv.at[k], target)
        c.start()
        return c


class RowSum:
    def __init__(self, net, src, far, got, both, up, down, by_up):
        self.net, self.src, self.far, self.got, self.both = net, src, far, got, both
        self.up, self.down, self.by_up = up, down, by_up

    def first(self):
        net, src = self.net, self.src
        if self.by_up:
            self.c = [net.start(src(2), self.far, self.up), net.start(src(3), self.got[1], self.down)]
        else:
            self.c = [net.start(src(2), self.far, self.down), net.start(src(1), self.got[0], self.up)]

    def second(self):
        self.c[0].wait_recv()
        t = self.src(1 if self.by_up else 3)[...].astype(F32) + self.far[...].astype(F32)
        self.both[...] = t.astype(BF)
        if self.by_up:
            self.c.append(self.net.start(self.both, self.got[0], self.up))
        else:
            self.c.append(self.net.start(self.both, self.got[1], self.down))

    def total(self):
        self.c[1].wait_recv()
        self.c[2].wait_recv()
        t = self.src(0)[...].astype(F32)
        return t + self.got[0][...].astype(F32) + self.got[1][...].astype(F32)

    def end(self):
        for c in self.c:
            c.wait_send()


def normalise(v):
    mean = jnp.mean(v, -1, keepdims=True)
    centered = v - mean
    rstd = lax.rsqrt(jnp.mean(centered * centered, -1, keepdims=True) + 1e-06)
    return centered * rstd, rstd


def turn(v, by):
    return jnp.concatenate([v[:, -by:], v[:, :-by]], 1)


def nt(a, b):
    return lax.dot_general(a, b, (((1,), (1,)), ((), ())), preferred_element_type=F32)


def tn(a, b):
    return lax.dot_general(a, b, (((0,), (0,)), ((), ())), preferred_element_type=F32)


def attention(qa, ka, va, da):
    scale = HEAD_DIM ** (-0.5)
    rows = lax.broadcasted_iota(jnp.int32, (256, 256), 0)
    cols = lax.broadcasted_iota(jnp.int32, (256, 256), 1)
    same = (rows & 7) == (cols & 7)
    outs = [[[] for _ in range(3)] for _ in range(4)]
    for head, (lo, hi) in enumerate(((0, 128), (0, 256), (128, 256), (128, 384))):
        lane = lax.broadcasted_iota(jnp.int32, (1, hi - lo), 1) + lo
        keep = (lane >= HEAD_DIM * head) & (lane < HEAD_DIM * (head + 1))
        q, k, v, d = (a[:, lo:hi] for a in (qa, ka, va, da))
        km = jnp.where(keep, k, jnp.zeros_like(k))
        vm = jnp.where(keep, v, jnp.zeros_like(v))
        scores = jnp.where(same, nt(km, q), -1e30)
        top = jnp.max(scores, 0, keepdims=True)
        e = jnp.exp2((scores - top) * (scale * LOG2E))
        probs = e * (1.0 / jnp.sum(e, 0, keepdims=True))
        probs_b = probs.astype(BF)
        att = tn(probs_b, v).astype(BF)
        dprobs = nt(vm, d)
        delta = jnp.sum(probs_b.astype(F32) * dprobs, 0, keepdims=True)
        ds = (probs * (dprobs - delta) * scale).astype(BF)
        dq = tn(ds, k)
        dk = jnp.dot(ds, q, preferred_element_type=F32)
        dv = jnp.dot(probs_b, d, preferred_element_type=F32)
        for slot, val in zip(outs, (dq, dk, dv, att.astype(F32))):
            val = jnp.where(keep, val, 0.0)
            for t in range(lo // 128, hi // 128):
                slot[t].append(val[:, t * 128 - lo : t * 128 - lo + 128])
    return [jnp.concatenate([functools.reduce(lambda a, b: a + b, t) for t in s], 1) for s in outs]


def kernel(
    in_hbm, up_hbm, gate_ref, wq_ref, wo_ref, out, gq, go,
    in_ref, up_ref, sib_v, away_v, mine_p, mine_q, nat_v, xg_v, perm_v, rstd_v, buf_p, buf_q, xin,
    w_v, g_v, f_v, dw_p, dw_q, dn, rs, ps, rh, res_v, og,
    far_p, got_p, both_p, pyp, rxp, pxp, rzp, rq, tq, zq, far_q, got_q, both_q, pq, rxq, fin_v, fsib_v,
    send_sem, recv_sem, o_send, o_recv, s_send, s_recv, l_sem,
):
    x, z, y, core, h = place()
    zl = z % 2
    ck = zl * 4 + y
    member = ck * 2 + core
    base = (x * 8 + (z // 2) * 2) * 8
    above, below, far = (y + 1) % 4, (y + 3) % 4, (y + 2) % 4
    sibling = (seq_of(x, z, y, 1 - core), h)
    x_peer = (seq_of(1 - x, z, y, core), h)
    h_peer = (seq_of(x, z, y, core), 1 - h)
    y_up = (seq_of(x, z, above, core), h)
    y_dn = (seq_of(x, z, below, core), h)
    z_up = (seq_of(x, (z + 1) % 8, y, core), h)
    z_dn = (seq_of(x, (z + 7) % 8, y, core), h)
    z_peers = [(seq_of(x, (z + d) % 8, y, core), h) for d in range(1, 8)]
    plane, other = pl.ds(zl * 4, 4), pl.ds((1 - zl) * 4, 4)
    zb = (z // 2) * 2
    near_peers = [(seq_of(x, z, yy, core), h) for yy in [(y + d) % 4 for d in range(1, 4)]]
    cross_peers = [(seq_of(x, zb + 1 - zl, yy, core), h) for yy in [(y + d) % 4 for d in range(4)]]
    group = [(base + (member + i) % 16, h) for i in range(1, 16)]
    everyone = [x_peer, h_peer] + z_peers + group
    net = Copies(send_sem, recv_sem)
    barrier = pltpu.get_barrier_semaphore()
    for peer in everyone:
        signal(barrier, peer)

    load = [
        pltpu.make_async_copy(in_hbm, in_ref, l_sem.at[2]),
        pltpu.make_async_copy(up_hbm, up_ref, l_sem.at[3]),
    ]
    for c in load:
        c.start()

    wq, wo = wq_ref[...].astype(F32), wo_ref[...].astype(F32)
    blocks = []
    for half in range(2):
        c = slice(288 * half, 288 * half + 288)
        rows = jnp.concatenate([wq[:, 0, c], wq[:, 1, c], wq[:, 2, c], wo[:, c]], 1)
        main, last = rows[0:8], rows[8:9]
        last = [last[:, 128 * j : 128 * j + 128] for j in range(9)] + [jnp.zeros((7, 128), F32)]
        last = jnp.concatenate(last, 0)
        main0 = jnp.concatenate([main, jnp.zeros((8, D), F32)], 0)
        main1 = jnp.concatenate([jnp.zeros((8, D), F32), main], 0)
        none = jnp.zeros((16, 128), F32)
        block0 = jnp.concatenate([main0, last, none], 1)
        block1 = jnp.concatenate([main1, none, last], 1)
        blocks.append(jnp.where(core == 0, block0, block1))
    away_v[...] = jnp.where(core == 0, blocks[1], blocks[0]).astype(BF)
    mine = jnp.where(core == 0, blocks[0], blocks[1])
    row = permuted_feature((D, 1), 0)
    col = lax.broadcasted_iota(jnp.int32, (1, D), 1)
    perm_v[...] = jnp.where(row == col, 1.0, 0.0).astype(BF)
    for c in load:
        c.wait()
    ghat, rstd = normalise(in_ref[...].reshape(256, D).astype(F32))
    rstd_v[...] = rstd
    nat_v[0] = ghat.astype(BF)
    nat_v[1] = (gate_ref[...].reshape(1, D) * up_ref[...].reshape(256, D).astype(F32)).astype(BF)
    pl.semaphore_wait(barrier, len(everyone))

    swap = net.start(away_v, sib_v, sibling)
    for i in range(2):
        p = jnp.dot(nat_v[i], perm_v[...], preferred_element_type=F32)
        for g in range(16):
            part = jnp.concatenate([p[8 * g : 8 * g + 8], p[128 + 8 * g : 136 + 8 * g]], 0)
            xg_v[g, :, i * D : (i + 1) * D] = part.astype(BF)
    swap.wait()
    mine = (mine + sib_v[...].astype(F32)).astype(BF)
    own_q = mine[:, GP:D]
    mine_p[:, 0:GP] = mine[:, :GP]
    mine_p[:, GP:GW] = mine[:, D:]
    mine_q[...] = own_q
    buf_p[x, 0, y, :, 0:GP] = mine[:, :GP]
    buf_p[x, 0, y, :, GP:GW] = mine[:, D:]
    buf_q[z, x, y] = own_q
    q_x = net.start(mine_q, buf_q.at[z, x, y], x_peer)
    sent = [{} for _ in GROUPS]

    def first(g):
        own = buf_p.at[x, GROUPS[g], y]
        for way, peer in (("up", y_up), ("dn", y_dn), ("x", x_peer)):
            sent[g][way] = net.start(own, own, peer)

    z_c = {}

    def z_send(d):
        z_c[d] = net.start(mine_p, buf_p.at[x, SLOT[8 - d], y], z_peers[d - 1])

    def arrived(g):
        for j in range(GROUPS[g].start, GROUPS[g].start + GROUPS[g].size):
            z_c[8 - OFFS[j]].wait_recv()

    def second(g):
        t = sent[g]
        t["up"].wait_recv()
        got = buf_p.at[x, GROUPS[g], below]
        t["f"] = net.start(got, got, y_up)
        t["x"].wait_recv()
        own = buf_p.at[1 - x, GROUPS[g], y]
        t["oup"] = net.start(own, own, y_up)
        t["odn"] = net.start(own, own, y_dn)

    def third(g):
        t = sent[g]
        t["odn"].wait_recv()
        got = buf_p.at[1 - x, GROUPS[g], above]
        t["of"] = net.start(got, got, y_dn)

    def pass_on(at, peer):
        return net.start(at, at, peer)

    tok, tok_z = {}, {}

    def tok_near(d):
        to = zl * 4 + (y + d) % 4
        tok[d] = net.start(xg_v.at[pl.ds(2 * to, 2)], xin.at[:, ck, core], near_peers[d - 1])

    def tok_cross(d):
        to = (1 - zl) * 4 + (y + d) % 4
        tok_z[d] = net.start(xg_v.at[2 * to + h], xin.at[h, ck, core], cross_peers[d])

    t_h = []

    def tok_share(d):
        tok_z[d].wait_recv()
        t_h.append(pass_on(xin.at[h, (1 - zl) * 4 + (y + 4 - d) % 4, core], h_peer))

    for d in (1, 7, 2, 6, 3, 5, 4):
        z_send(d)
    first(0)
    own_t = pltpu.make_async_copy(xg_v.at[pl.ds(2 * ck, 2)], xin.at[:, ck, core], l_sem.at[0])
    own_t.start()
    q_x.wait_recv()
    q_c = [pass_on(buf_q.at[z, :, y], y_up), pass_on(buf_q.at[z, :, y], y_dn)]
    arrived(1)
    first(1)
    q_c[0].wait_recv()
    q_f0 = pass_on(buf_q.at[z, 0, below], y_up)
    q_c[1].wait_recv()
    q_f1 = pass_on(buf_q.at[z, 1, above], y_dn)
    tok_cross(0)
    tok_cross(2)
    arrived(2)
    first(2)
    second(0)
    q_f0.wait_recv()
    q_f1.wait_recv()
    ring_up, ring_dn = [[], []], [[], []]
    for i in range(2):
        ring_up[i].append(pass_on(buf_q.at[z, i], z_up))
        ring_dn[i].append(pass_on(buf_q.at[z, i], z_dn))

    def ring(step):
        for i in range(2):
            ring_up[i][-1].wait_recv()
            if step < 3 or i == 0:
                ring_up[i].append(pass_on(buf_q.at[(z + 8 - step) % 8, i], z_up))
            ring_dn[i][-1].wait_recv()
            if step < 3 or i == 1:
                ring_dn[i].append(pass_on(buf_q.at[(z + step) % 8, i], z_dn))

    tok_cross(1)
    tok_cross(3)
    arrived(3)
    first(3)
    second(1)
    tok_near(1)
    tok_near(3)
    tok_share(0)
    tok_share(2)
    ring(1)
    third(0)
    second(2)
    tok_near(2)
    tok_share(1)
    tok_share(3)
    third(1)
    ring(2)
    second(3)
    own_t.wait()
    for d in (1, 3, 2):
        tok[d].wait_recv()
    t_s = [pass_on(xin.at[:, plane, core], sibling)]
    third(2)
    for c in t_h:
        c.wait_recv()
    t_s.append(pass_on(xin.at[:, other, core], sibling))
    ring(3)
    third(3)
    for g, t in enumerate(sent):
        for name in ("dn", "f", "of", "oup"):
            t[name].wait_recv()
    for xx in range(2):
        for j in range(8):
            k = pl.ds(pl.multiple_of((xx * 8 + (z + OFFS[j]) % 8) * 64, 64), 64)
            w_v[k, 0:GP] = buf_p[xx, j, :, :, 0:GP].reshape(64, GP)
    for r in range(2):
        for xx in range(2):
            for j in range(8):
                k = pl.ds(pl.multiple_of((xx * 8 + (z + OFFS[j]) % 8) * 64, 64), 64)
                part = buf_p[xx, j, :, :, GP + 128 * r : GP + 128 * (r + 1)]
                f_v[k, :] = part.reshape(64, 128).astype(F32)
        for j in range(9):
            w_v[1024 + 64 * r : 1088 + 64 * r, 128 * j : 128 * (j + 1)] = f_v[
                pl.ds(j, 64, stride=16), :
            ].astype(BF)
    ring_up[0][-1].wait_recv()
    ring_dn[1][-1].wait_recv()
    for xx in range(2):
        for zz in range(8):
            k = (xx * 8 + zz) * 64
            w_v[k : k + 64, GP:D] = buf_q[zz, xx].reshape(64, GQ)
    for c in t_s:
        c.wait_recv()

    lane = lax.broadcasted_iota(jnp.int32, (1, 896), 1)
    away = pl.ds(pl.multiple_of((1 - core) * 128, 128), 128)
    here = pl.ds(pl.multiple_of(core * 128, 128), 128)

    def swap_dn(pg):
        return remote(dn.at[pg, away], rs.at[pg], s_send.at[pg], s_recv.at[pg], sibling)

    def tokens(pg):
        tok = slice(pg * 256, pg * 256 + 256)
        src = xin[pg].reshape(256, 2 * D)
        qkv = jnp.dot(src[:, :D], w_v[:, 0:896], preferred_element_type=F32)
        od = jnp.dot(src[:, D:], w_v[:, 768:1152], preferred_element_type=F32)
        qa = qkv[:, 0:384].astype(BF)
        ka = turn(qkv[:, 256:640], -32).astype(BF)
        va = turn(qkv[:, 512:896], -64).astype(BF)
        da = turn(od, -96).astype(BF)
        dq, dk, dv, att = attention(qa, ka, va, da)
        dk, dv, att = turn(dk, 32), turn(dv, 64), turn(att, 96)
        tiles = [[] for _ in range(9)]
        for start, val in ((0, dq), (2, dk), (4, dv), (6, att)):
            for t in range(3):
                tiles[start + t].append(val[:, 128 * t : 128 * (t + 1)])
        for t in range(9):
            g_v[tok, 128 * t : 128 * (t + 1)] = functools.reduce(lambda a, b: a + b, tiles[t]).astype(BF)

    tokens(0)
    tokens(1)

    def grads(i):
        a = tn(xin[:, :, :, :, pl.ds(pl.multiple_of(128 * i, 128), 128)].reshape(512, 128), g_v[:, 0:896])
        b = tn(
            xin[:, :, :, :, pl.ds(pl.multiple_of(D + 128 * i, 128), 128)].reshape(512, 128),
            g_v[:, 768:1152],
        )
        lane = lax.broadcasted_iota(jnp.int32, (1, 128), 1)
        mid = jnp.where(lane < 96, a[:, 768:896], b[:, 0:128])
        return jnp.concatenate([a[:, 0:768], mid, b[:, 128:384]], 1)

    def grad_rows(i, carry):
        block = grads(i).astype(BF).reshape(2, 4, 16, D)
        xx = i // 4
        for e in range(2):
            zz = 2 * (i % 4) + e
            o = (zz + 8 - z) % 8
            slot = (o // 4) * (15 - 4 * o) + 2 * o
            dw_p[xx, slot, :, :, 0:SP] = block[e, :, :, :SP]
            dw_q[zz, xx] = block[e, :, :, SP:]
        return carry

    lax.fori_loop(0, 8, grad_rows, 0)

    def q_own(o):
        return dw_q.at[(z + o) % 8]

    q_ring = {(0, 0): [net.start(dw_q.at[(z + 4) % 8, 0], rq.at[0, 0, 0], z_up)]}
    q_ring[1, 1] = [net.start(dw_q.at[(z + 4) % 8, 1], rq.at[1, 0, 1], z_dn)]
    for i, o, peer in ((0, 3, z_up), (1, 5, z_dn)):
        q_ring[i, 1 - i] = [net.start(dw_q.at[(z + o) % 8, 1 - i], rq.at[i, 1, 1 - i], peer)]

    def q_step(s):
        for i, o, peer in ((0, 4 - s, z_up), (1, 4 + s, z_dn)):
            for half in (i, 1 - i):
                if s == 1 and half != i:
                    continue
                q_ring[i, half][-1].wait_recv()
                t = q_own(o)[half].astype(F32) + rq[i, s - 1, half].astype(F32)
                tq[i, s - 1, half] = t.astype(BF)
                q_ring[i, half].append(net.start(tq.at[i, s - 1, half], rq.at[i, s, half], peer))

    rest = grads(8)
    for r in range(2):
        f_v[...] = jnp.zeros((1024, 128), F32)
        for j in range(9):
            f_v[pl.ds(j, 64, stride=16), :] = rest[64 * r : 64 * r + 64, 128 * j : 128 * (j + 1)]
        for xx in range(2):
            for j in range(8):
                k = pl.ds(pl.multiple_of((xx * 8 + (z + OFFS[j]) % 8) * 64, 64), 64)
                dw_p[xx, j, :, :, SP + 128 * r : SP + 128 * (r + 1)] = (
                    f_v[k, :].astype(BF).reshape(4, 16, 128)
                )

    sums = {}
    for g in (3, 2, 1, 0):
        for i, xx in enumerate((1 - x, x)):
            at = GROUPS[g]
            sums[g, i] = RowSum(
                net, (lambda d, xx=xx, at=at: dw_p.at[xx, at, (y + d) % 4]),
                far_p.at[i, at], (got_p.at[i, 0, at], got_p.at[i, 1, at]), both_p.at[i, at],
                y_up, y_dn, i == 0,
            )

    def y_first(g):
        for i in range(2):
            sums[g, i].first()

    def y_second(g):
        for i in range(2):
            sums[g, i].second()

    x_c, z_s = {}, {}

    def y_total(g):
        at = GROUPS[g]
        pyp[0, at] = sums[g, 0].total().astype(BF)
        x_c[g] = net.start(pyp.at[0, at], rxp.at[at], x_peer)
        pyp[1, at] = sums[g, 1].total().astype(BF)

    def x_total(g):
        at = GROUPS[g]
        x_c[g].wait_recv()
        pxp[at] = (pyp[1, at].astype(F32) + rxp[at].astype(F32)).astype(BF)
        for j in range(at.start, at.start + at.size):
            if j:
                z_s[j] = net.start(pxp.at[j], rzp.at[j - 1], z_peers[OFFS[j] - 1])

    def partial_dn(pg):
        left = jnp.where(lane < 864, g_v[pg * 256 : pg * 256 + 256, 0:896], jnp.zeros((256, 896), BF))
        dn[pg] = nt(left, w_v[:, 0:896]).astype(BF)
        swap_dn(pg).start()

    y_first(3)
    y_first(2)
    partial_dn(0)
    partial_dn(1)
    q_step(1)
    y_second(3)
    y_first(1)
    for pg in range(2):
        swap_dn(pg).wait_recv()
    ps[...] = (dn[:, here].astype(F32) + rs[...].astype(F32)).astype(BF)
    dn_h = net.start(ps.at[1 - h], rh, h_peer)
    q_step(2)
    y_second(2)
    y_total(3)
    y_first(0)
    y_second(1)
    dn_h.wait_recv()
    mine = ps[h].astype(F32) + rh[...].astype(F32)
    mine = mine.astype(BF).astype(F32)
    ghat = xin[h, pl.ds(4 * core, 4), :, :, 0:D].reshape(128, D).astype(F32)
    one = jnp.mean(mine, -1, keepdims=True)
    two = jnp.mean(mine * ghat, -1, keepdims=True)
    res_v[...] = (mine - one - ghat * two).astype(BF).reshape(8, 16, D)

    local = zl == core

    def owner(i):
        to = (member + i) % 8
        target = (base + 8 * core + to, h)
        return remote(res_v.at[to], og.at[ck, h], o_send.at[i], o_recv.at[ck], target)

    stay = pltpu.make_async_copy(res_v.at[member % 8], og.at[ck, h], l_sem.at[1])
    pl.when(jnp.logical_not(local))(lambda: owner(0).start())
    pl.when(local)(lambda: stay.start())
    for i in range(1, 8):
        owner(i).start()

    q_step(3)
    y_total(2)
    x_total(3)
    y_second(0)

    def out_share(part):
        for c in range(4 * part, 4 * part + 4):
            got = remote(res_v.at[0], og.at[c, h], o_send.at[0], o_recv.at[c], h_peer)
            pl.when(jnp.logical_not(local & (ck == c)))(lambda got=got: got.wait_recv())
            pl.when(local & (ck == c))(lambda: stay.wait())
        at = og.at[pl.ds(4 * part, 4), h]
        return net.start(at, at, h_peer)

    y_total(1)
    o_h = [out_share(0)]
    x_total(2)
    y_total(0)
    o_h.append(out_share(1))
    for c in q_ring.values():
        c[-1].wait_recv()
    t = q_own(0)[...].astype(F32) + rq[0, 3].astype(F32) + rq[1, 3].astype(F32)
    zq[...] = t.astype(BF)
    q_sums = []
    for i in range(2):
        at = pl.ds(i, 1)
        q_sums.append(
            RowSum(
                net, (lambda d, at=at: zq.at[at, (y + d) % 4]),
                far_q.at[at], (got_q.at[0, at], got_q.at[1, at]), both_q.at[at],
                y_up, y_dn, i == 0,
            )
        )
        q_sums[i].first()
    x_total(1)
    for i in range(2):
        q_sums[i].second()
    x_total(0)
    for i in range(2):
        pq[i] = q_sums[i].total()[0].astype(BF)
    q_x2 = net.start(pq.at[1 - x], rxq, x_peer)

    t = pxp[0].astype(F32)
    for j in range(1, 8):
        z_s[j].wait_recv()
        t = t + rzp[j - 1].astype(F32)
    fin_v[:, 0:SP] = t[:, :SP]
    fin_v[:, D:BLK] = t[:, SP:]
    q_x2.wait_recv()
    fin_v[:, SP:D] = pq[x].astype(F32) + rxq[...].astype(F32)
    last = net.start(fin_v, fsib_v, sibling)
    for c in o_h:
        c.wait_recv()
    back = nt(og[...].reshape(256, D), perm_v[...])
    for f in range(2):
        nat = jnp.concatenate([back[16 * g + 8 * f : 16 * g + 8 * f + 8] for g in range(16)], 0)
        nat = up_ref[f].astype(F32) + rstd_v[128 * f : 128 * f + 128] * nat
        out[f] = nat.astype(BF)

    last.wait()

    mine, other = fin_v[...], fsib_v[...]
    rows = []
    for half in (jnp.where(core == 0, mine, other), jnp.where(core == 0, other, mine)):
        main = jnp.where(core == 0, half[0:8, :D], half[8:16, :D])
        tail = jnp.where(core == 0, half[0:9, D : D + 128], half[0:9, D + 128 :])
        tail = jnp.concatenate([tail[j : j + 1] for j in range(9)], 1)
        rows.append(jnp.concatenate([main, tail], 0))
    for t in range(4):
        both = jnp.concatenate([r[:, 288 * t : 288 * t + 288] for r in rows], 1)
        if t < 3:
            gq[:, t, :] = both
        else:
            go[...] = both

    pl.when(jnp.logical_not(local))(lambda: owner(0).wait_send())
    for i in range(1, 8):
        owner(i).wait_send()
    for pg in range(2):
        swap_dn(pg).wait_send()
    for t in sent:
        for c in t.values():
            c.wait_send()
    rest = o_h + [q_x, q_f0, q_f1, dn_h, q_x2] + q_c + t_h + t_s
    for c in ring_up + ring_dn + list(q_ring.values()):
        rest = rest + c
    for c in rest + list(tok.values()) + list(tok_z.values()) + list(z_c.values()) + list(x_c.values()) + list(z_s.values()):
        c.wait_send()
    for c in q_sums + list(sums.values()):
        c.end()


def on_device(inputs, out_grad, gate, qkv_weight, out_weight):
    vm = pl.BlockSpec(memory_space=pltpu.VMEM)
    hbm = pl.BlockSpec(memory_space=pl.ANY)
    dma = pltpu.SemaphoreType.DMA
    shape = jax.ShapeDtypeStruct
    bf = lambda *dims: pltpu.VMEM(dims, BF)
    f32 = lambda *dims: pltpu.VMEM(dims, F32)
    grad_inputs, grad_qkv, grad_out = pl.pallas_call(
        kernel,
        out_shape=[shape((2, 128, D), BF), shape((9, 3, 576), F32), shape((9, 576), F32)],
        in_specs=[hbm] * 2 + [vm] * 3,
        out_specs=[vm] * 3,
        scratch_shapes=[
            bf(2, 128, D), bf(2, 128, D),
            bf(16, BLK), bf(16, BLK), bf(16, GW), bf(16, GQ), bf(2, 256, D), bf(16, 16, 2 * D), bf(D, D),
            f32(256, 1), bf(XS, ZS, YS, 16, GW), bf(ZS, XS, YS, 16, GQ), bf(2, 8, 2, 16, 2 * D),
            bf(D, D), bf(512, D), f32(1024, 128), bf(XS, ZS, YS, 16, SW), bf(ZS, XS, YS, 16, SQ),
            bf(2, 256, D), bf(2, 128, D), bf(2, 128, D), bf(128, D), bf(8, 16, D), bf(8, 2, 16, D),
            bf(2, ZS, 16, SW), bf(2, 2, ZS, 16, SW), bf(2, ZS, 16, SW), bf(2, ZS, 16, SW),
            bf(ZS, 16, SW), bf(ZS, 16, SW), bf(7, 16, SW),
            bf(2, 4, XS, YS, 16, SQ), bf(2, 3, XS, YS, 16, SQ), bf(XS, YS, 16, SQ),
            bf(2, 16, SQ), bf(2, 2, 16, SQ), bf(2, 16, SQ), bf(2, 16, SQ), bf(16, SQ),
            f32(16, BLK), f32(16, BLK),
            dma((150,)), dma((150,)), dma((8,)), dma((8,)), dma((2,)), dma((2,)), dma((4,)),
        ],
        compiler_params=pltpu.CompilerParams(
            collective_id=0, has_side_effects=True, vmem_limit_bytes=VMEM_BYTES
        ),
        name="sublayer_backward",
    )(inputs, out_grad, gate, qkv_weight, out_weight)
    return grad_inputs, grad_qkv, grad_out


def solution(mesh):
    in_specs = (
        P("seq", None, None),
        P("seq", None, None),
        P(),
        P("seq", None, "head"),
        P("seq", "head"),
    )
    out_specs = (P("seq", None, None), P("seq", None, "head"), P("seq", "head"))
    return jax.shard_map(
        on_device, mesh=mesh, in_specs=in_specs, out_specs=out_specs, check_vma=False
    )
```
